32 devices in a mesh: row: 4 (over x, core), col: 4 (over z), depth: 2 (over y).
Axes of the slice: x: 2, y: 2, z: 4, core: 2. Of those that a mesh axis runs over, the one named last changes fastest.
Arguments:
- tokens: bfloat16 [768, 3072], P(('col', 'depth'), 'row'), may hold values from -6 to 6
- weight_in: bfloat16 [3072, 12288], P('row', 'col'), may hold values from -0.109375 to 0.109375
- weight_out: bfloat16 [12288, 3072], P('col', 'row'), may hold values from -0.0546875 to 0.0546875
- output_grad: bfloat16 [768, 3072], P(('col', 'depth'), 'row'), may hold values from -6 to 6
Outputs:
- output: bfloat16 [768, 3072], P(('col', 'depth'), 'row')
- input_grad: bfloat16 [768, 3072], P(('col', 'depth'), 'row')
- weight_in_grad: float32 [3072, 12288], P(('row', 'depth'), 'col')
- weight_out_grad: float32 [12288, 3072], P(('col', 'depth'), 'row')
The draws below stay inside these ranges and needn't reach their ends.
All inputs are finite; a program needn't handle non-finite values.
Results may differ from the reference program's by a relative error of at most 0.018.
Values may be sent and summed in bfloat16 or wider, within the bound.
No kernel may reach another device: no remote copies, remote signals or barrier semaphores. Data moves between devices by JAX's collectives and lax.ppermute only.
A program may use at most 128 MiB of HBM per device.

```python
import jax
import jax.numpy as jnp
from jax import lax

D = 3072
FF = 12288
TOKENS = 768
N_ROW = 4
N_COL = 4
N_DEPTH = 2


def level_of(rng, dims, shards, smallest, high):
    gain, own = 1.0, jax.random.fold_in(rng, 6)
    for position, shards_of in shards:
        heights = jnp.exp(jax.random.uniform(jax.random.fold_in(own, position), (shards_of,), jnp.float32, smallest / len(shards), high / len(shards)))
        gain = gain * jnp.repeat(heights, dims[position] // shards_of).reshape([-1 if axis == position else 1 for axis in range(len(dims))])
    return gain


def centred(key, dims, scale, bound, shards=(), kind=jnp.bfloat16):
    loudness = level_of(key, dims, shards, -0.22, 0.18) if shards else 1.0
    array = jax.random.normal(key, dims, jnp.float32) * scale * loudness
    return jnp.minimum(jnp.maximum(array, -bound), bound).astype(kind)


def setup_inputs(seed: int = 0) -> dict:
    seeds = jax.random.split(jax.random.key(seed), 5)
    return {
        "tokens": centred(seeds[0], (TOKENS, D), 1.0, 6.0, ((0, 8), (1, 4))),
        "weight_in": centred(seeds[1], (D, FF), D ** -0.5, 0.109375, ((0, 4), (1, 4))),
        "weight_out": centred(seeds[2], (FF, D), FF ** -0.5, 0.0546875, ((0, 4), (1, 4))),
        "output_grad": centred(seeds[3], (TOKENS, D), 1.0, 6.0, ((0, 8), (1, 4))),
    }


def split_product(left_side, right_side, parts):
    block_width = left_side.shape[1] // parts

    def block_step(total, block_index):
        left_block = lax.dynamic_slice_in_dim(left_side, block_index * block_width, block_width, 1)
        right_block = lax.dynamic_slice_in_dim(right_side, block_index * block_width, block_width, 0)
        partial_value = jnp.dot(left_block, right_block, preferred_element_type=jnp.float32)
        rounded = lax.optimization_barrier(partial_value.astype(jnp.bfloat16)).astype(jnp.float32)
        return total + rounded, None

    start_total = jnp.zeros((left_side.shape[0], right_side.shape[1]), jnp.float32)
    total, _ = lax.scan(block_step, start_total, jnp.arange(parts, dtype=jnp.int32))
    return total


def gelu_parts(hidden_pre):
    normal_cdf = 0.5 * (1.0 + lax.erf(hidden_pre * 0.7071067811865476))
    normal_pdf = jnp.exp(-0.5 * hidden_pre * hidden_pre) * 0.3989422804014327
    return hidden_pre * normal_cdf, normal_cdf + hidden_pre * normal_pdf


def group_order(values):
    block_rows = TOKENS // (N_COL * N_DEPTH)
    shaped = values.reshape(N_COL, N_DEPTH, block_rows, values.shape[1])
    return jnp.transpose(shaped, (1, 0, 2, 3)).reshape(TOKENS, values.shape[1])


def reference(tokens, weight_in, weight_out, output_grad):
    hidden_pre = split_product(tokens, weight_in, N_ROW)
    gelu_value, gelu_slope = gelu_parts(hidden_pre)
    activation = gelu_value.astype(jnp.bfloat16)
    output = split_product(activation, weight_out, N_COL).astype(jnp.bfloat16)
    act_grad = split_product(output_grad, weight_out.T, N_ROW)
    pre_grad = (act_grad * gelu_slope).astype(jnp.bfloat16)
    input_grad = split_product(pre_grad, weight_in.T, N_COL).astype(jnp.bfloat16)
    weight_in_grad = split_product(group_order(tokens).T, group_order(pre_grad), N_DEPTH)
    weight_out_grad = split_product(group_order(activation).T, group_order(output_grad), N_DEPTH)
    return output, input_grad, weight_in_grad, weight_out_grad
```

```python
import functools

import jax
import jax.numpy as jnp
from jax import lax
from jax.experimental import pallas as pl
from jax.experimental.pallas import tpu as pltpu
from jax.sharding import PartitionSpec as P

BF16, F32 = jnp.bfloat16, jnp.float32
VMEM_LIMIT = 32 * 1024 * 1024


def gelu_parts(hidden_pre):
    normal_cdf = 0.5 * (1.0 + lax.erf(hidden_pre * 0.7071067811865476))
    normal_pdf = jnp.exp(-0.5 * hidden_pre * hidden_pre) * 0.3989422804014327
    return (hidden_pre * normal_cdf, normal_cdf + hidden_pre * normal_pdf)


def dot(left, right, left_dim, right_dim):
    return lax.dot_general(
        left, right, (((left_dim,), (right_dim,)), ((), ())), preferred_element_type=F32
    )


def call(kernel, grid, in_specs, out_specs, out_shape, scratch, flops, bytes_accessed):
    return pl.pallas_call(
        kernel,
        grid_spec=pltpu.PrefetchScalarGridSpec(
            num_scalar_prefetch=1,
            grid=grid,
            in_specs=in_specs,
            out_specs=out_specs,
            scratch_shapes=scratch,
        ),
        out_shape=out_shape,
        compiler_params=pltpu.CompilerParams(vmem_limit_bytes=VMEM_LIMIT),
        cost_estimate=pl.CostEstimate(
            flops=flops, bytes_accessed=bytes_accessed, transcendentals=0
        ),
    )


def hidden_kernel(blocks, where, tokens, cotangent, weight_in, weight_out, *outs):
    step = pl.program_id(0)
    other_hidden, other_grad, own_hidden, own_grad = outs
    hidden = dot(tokens[...], weight_in[...], 1, 0).astype(BF16)
    grad = dot(cotangent[...], weight_out[...], 1, 1).astype(BF16)

    @pl.when(step < blocks)
    def _():
        other_hidden[...] = hidden
        other_grad[...] = grad

    @pl.when(step >= blocks)
    def _():
        own_hidden[...] = hidden
        own_grad[...] = grad


def hidden_partials(where, tokens, cotangent, weight_in, weight_out):
    rows, features = tokens.shape
    half = weight_in.shape[1] // 2
    blocks = 2
    width = half // blocks

    def place(step, where):
        core = jnp.where(step < blocks, 1 - where[0], where[0])
        return core * blocks + step % blocks

    whole = pl.BlockSpec((rows, features), lambda step, where: (0, 0))
    other = pl.BlockSpec((rows, width), lambda step, where: (0, jnp.minimum(step, blocks - 1)))
    own = pl.BlockSpec((rows, width), lambda step, where: (0, jnp.maximum(step - blocks, 0)))
    return call(
        functools.partial(hidden_kernel, blocks),
        (2 * blocks,),
        [
            whole,
            whole,
            pl.BlockSpec((features, width), lambda step, where: (0, place(step, where))),
            pl.BlockSpec((width, features), lambda step, where: (place(step, where), 0)),
        ],
        [other, other, own, own],
        [jax.ShapeDtypeStruct((rows, half), BF16)] * 4,
        [],
        8 * rows * features * half,
        8 * features * half + 12 * rows * half,
    )(where, tokens, cotangent, weight_in, weight_out)


def model_kernel(ring, where, *refs):
    step = pl.program_id(0)
    own_act, own_pre, other_act, other_pre, out_a, in_a, out_b, in_b = refs[:8]
    arrived = refs[8:10] if ring else ()
    out, grad, out_sum, grad_sum = refs[-4:]
    new_out = dot(own_act[...], out_a[...], 1, 0) + dot(other_act[...], out_b[...], 1, 0)
    new_grad = dot(own_pre[...], in_a[...], 1, 1) + dot(other_pre[...], in_b[...], 1, 1)

    @pl.when(step == 0)
    def _():
        out_sum[...] = new_out
        grad_sum[...] = new_grad

    @pl.when(step > 0)
    def _():
        out_sum[...] += new_out
        grad_sum[...] += new_grad

    @pl.when(step == pl.num_programs(0) - 1)
    def _():
        if ring:
            out[...] = (out_sum[...] + arrived[0][...].astype(F32)).astype(BF16)
            grad[...] = (grad_sum[...] + arrived[1][...].astype(F32)).astype(BF16)
        else:
            out[...] = out_sum[...].astype(BF16)
            grad[...] = grad_sum[...].astype(BF16)


def model_partials(where, own, other, weight_in, weight_out, arrived):
    rows, half = own[0].shape
    features = weight_in.shape[0]
    blocks = 2
    width = half // blocks
    block = pl.BlockSpec((rows, width), lambda step, where: (0, step))
    whole = pl.BlockSpec((rows, features), lambda step, where: (0, 0))

    def weights(core):
        return [
            pl.BlockSpec((width, features), lambda step, where: (core(where) * blocks + step, 0)),
            pl.BlockSpec((features, width), lambda step, where: (0, core(where) * blocks + step)),
        ]

    return call(
        functools.partial(model_kernel, bool(arrived)),
        (blocks,),
        [block] * 4
        + weights(lambda where: where[0])
        + weights(lambda where: 1 - where[0])
        + [whole] * len(arrived),
        [whole, whole],
        [jax.ShapeDtypeStruct((rows, features), BF16)] * 2,
        [pltpu.VMEM((rows, features), F32)] * 2,
        8 * rows * features * half,
        8 * features * half + 8 * rows * half,
    )(where, *own, *other, weight_out, weight_in, weight_out, weight_in, *arrived)


def weight_kernel(chunks, blocks, pieces, before, where, *refs):
    step = pl.program_id(0)
    tokens, cotangents = refs[:chunks], refs[chunks : 2 * chunks]
    own_pre, other_pre = refs[2 * chunks : 3 * chunks], refs[3 * chunks : 4 * chunks]
    own_act, other_act = refs[4 * chunks : 5 * chunks], refs[5 * chunks : 6 * chunks]
    earlier = refs[6 * chunks : 6 * chunks + 2] if before else ()
    in_grad, out_grad, all_tokens, all_cotangents, all_pre, all_act = refs[-6:]
    rows = tokens[0].shape[0]

    def fill(target, sources):
        for index, source in enumerate(sources):
            target[index * rows : (index + 1) * rows, :] = source[...]

    @pl.when(step == 0)
    def _():
        fill(all_tokens, tokens)
        fill(all_cotangents, cotangents)

    @pl.when(step < blocks)
    def _():
        fill(all_pre, own_pre)

    @pl.when(step >= blocks)
    def _():
        fill(all_pre, other_pre)

    new_in = dot(all_tokens[...], all_pre[...], 0, 0)
    if before:
        new_in += earlier[0][...].astype(F32)
    in_grad[...] = new_in.astype(in_grad.dtype)

    @pl.when(step < pieces)
    def _():
        @pl.when(where[2] == 1)
        def _():
            fill(all_act, own_act)

        @pl.when(where[2] == 0)
        def _():
            fill(all_act, other_act)

        new_out = dot(all_act[...], all_cotangents[...], 0, 0)
        if before:
            new_out += earlier[1][...].astype(F32)
        out_grad[...] = new_out.astype(out_grad.dtype)


def weight_terms(where, tokens, cotangents, pre, act, before, kind):
    chunks = len(tokens)
    rows, part = tokens[0].shape
    features = cotangents[0].shape[1]
    half = pre[0][0].shape[1]
    share = act[0][0].shape[1]
    blocks = 2
    width = half // blocks
    pieces = 2 * blocks if share % (256 * blocks) == 0 else 1
    piece = share // pieces

    def column(step, where):
        core = jnp.where(step < blocks, where[0], 1 - where[0])
        return core * blocks + step % blocks

    in_block = pl.BlockSpec((part, width), lambda step, where: (0, column(step, where)))
    out_block = pl.BlockSpec(
        (piece, features), lambda step, where: (jnp.minimum(step, pieces - 1), 0)
    )
    act_block = pl.BlockSpec((rows, piece), lambda step, where: (0, jnp.minimum(step, pieces - 1)))
    own_block = pl.BlockSpec((rows, width), lambda step, where: (0, jnp.minimum(step, blocks - 1)))
    other_block = pl.BlockSpec(
        (rows, width), lambda step, where: (0, jnp.maximum(step - blocks, 0))
    )
    return call(
        functools.partial(weight_kernel, chunks, blocks, pieces, bool(before)),
        (2 * blocks,),
        [pl.BlockSpec((rows, part), lambda step, where: (0, 0))] * chunks
        + [pl.BlockSpec((rows, features), lambda step, where: (0, 0))] * chunks
        + [own_block] * chunks
        + [other_block] * chunks
        + [act_block] * (2 * chunks)
        + ([in_block, out_block] if before else []),
        [in_block, out_block],
        [
            jax.ShapeDtypeStruct((part, 2 * half), kind),
            jax.ShapeDtypeStruct((share, features), kind),
        ],
        [
            pltpu.VMEM((chunks * rows, part), BF16),
            pltpu.VMEM((chunks * rows, features), BF16),
            pltpu.VMEM((chunks * rows, width), BF16),
            pltpu.VMEM((chunks * rows, piece), BF16),
        ],
        2 * chunks * rows * (2 * part * half + share * features),
        2 * chunks * rows * (part + features + 2 * half + share) + 8 * part * half + 4 * share * features,
    )(
        where,
        *tokens,
        *cotangents,
        *[pair[0] for pair in pre],
        *[pair[1] for pair in pre],
        *[pair[0] for pair in act],
        *[pair[1] for pair in act],
        *before,
    )


def shards(n_row, n_col, n_depth, tokens, weight_in, weight_out, output_grad):
    core = lax.axis_index("row") % 2
    depth = lax.axis_index("depth")
    half = weight_in.shape[1] // 2
    share = weight_in.shape[1] // n_depth
    part = tokens.shape[1] // n_depth
    halves = max(n_depth // 2, 1)
    where = jnp.stack([core, depth, (core == depth // halves).astype(jnp.int32)]).astype(jnp.int32)

    def swap_cores(value):
        return lax.ppermute(value, "row", [(r, r ^ 1) for r in range(n_row)])

    def to_chip(value, k):
        return lax.ppermute(value, "row", [(r, (r + 2 * k) % n_row) for r in range(n_row)])

    def to_depth(value, k):
        return lax.ppermute(value, "depth", [(d, (d + k) % n_depth) for d in range(n_depth)])

    def to_next(value):
        return lax.ppermute(value, "col", [(c, (c + 1) % n_col) for c in range(n_col)])

    def hidden_share(value, owner):
        if share == half:
            return value
        return lax.dynamic_slice_in_dim(value, (owner % halves) * share, share, 1)

    def feature_part(value, owner):
        return lax.dynamic_slice_in_dim(value, owner * part, part, 1)

    ring = [(tokens, output_grad)]
    for _ in range(n_col - 1):
        ring.append(tuple(to_next(value) for value in ring[-1]))

    own_tokens, own_cotangents, own_pre, own_act = [], [], [], []
    far = {k: ([], [], [], []) for k in range(1, n_depth)}
    kept, arrived = None, ()
    for stage, (panel, cotangent) in enumerate(ring):
        other_hidden, other_grad, mine_hidden, mine_grad = hidden_partials(
            where, panel, cotangent, weight_in, weight_out
        )
        chip_hidden = (mine_hidden.astype(F32) + swap_cores(other_hidden).astype(F32)).astype(BF16)
        chip_grad = (mine_grad.astype(F32) + swap_cores(other_grad).astype(F32)).astype(BF16)
        hidden, grad = chip_hidden.astype(F32), chip_grad.astype(F32)
        for k in range(1, n_row // 2):
            hidden += to_chip(chip_hidden, k).astype(F32)
            grad += to_chip(chip_grad, k).astype(F32)
        value, slope = gelu_parts(hidden)
        act, pre = value.astype(BF16), (grad * slope).astype(BF16)
        other_act, other_pre = swap_cores(act), swap_cores(pre)

        own_tokens.append(feature_part(panel, depth))
        own_cotangents.append(cotangent)
        own_pre.append((pre, other_pre))
        own_act.append((hidden_share(act, depth), hidden_share(other_act, depth)))

        for k in range(1, n_depth):
            target = (depth + k) % n_depth
            far_tokens, far_cotangents, far_pre, far_act = far[k]
            far_tokens.append(to_depth(feature_part(panel, target), k))
            far_cotangents.append(to_depth(cotangent, k))
            came = to_depth(pre, k)
            far_pre.append((came, swap_cores(came)))
            pairs = [
                (r * n_depth + d, r * n_depth + (d + k) % n_depth)
                for r in range(n_row)
                for d in range(n_depth)
                if r % 2 == (d + k) % n_depth // halves
            ]
            came = lax.ppermute(hidden_share(act, target), ("row", "depth"), pairs)
            pairs = [
                (r * n_depth + d, (r ^ 1) * n_depth + d)
                for r in range(n_row)
                for d in range(n_depth)
                if r % 2 == d // halves
            ]
            far_act.append((came, lax.ppermute(came, ("row", "depth"), pairs)))

        sums = model_partials(
            where, (act, pre), (other_act, other_pre), weight_in, weight_out, arrived
        )
        if stage == 0:
            kept = sums
        else:
            arrived = tuple(to_next(value) for value in sums)

    output, input_grad = (
        (mine.astype(F32) + came.astype(F32)).astype(BF16) for mine, came in zip(kept, arrived)
    )
    last = n_depth - 1
    terms = weight_terms(
        where, own_tokens, own_cotangents, own_pre, own_act, (), BF16 if last else F32
    )
    for k in range(1, n_depth):
        terms = weight_terms(where, *far[k], terms, F32 if k == last else BF16)
    return (output, input_grad, *terms)


def solution(mesh):
    placed = (
        P(("col", "depth"), "row"),
        P("row", "col"),
        P("col", "row"),
        P(("col", "depth"), "row"),
    )
    sizes = (mesh.shape["row"], mesh.shape["col"], mesh.shape["depth"])
    return jax.shard_map(
        functools.partial(shards, *sizes),
        mesh=mesh,
        in_specs=placed,
        out_specs=(
            P(("col", "depth"), "row"),
            P(("col", "depth"), "row"),
            P(("row", "depth"), "col"),
            P(("col", "depth"), "row"),
        ),
        check_vma=False,
    )
```

```python
import functools

import jax
import jax.numpy as jnp
from jax import lax
from jax.experimental import pallas as pl
from jax.experimental.pallas import tpu as pltpu
from jax.sharding import PartitionSpec as P

BF16, F32 = jnp.bfloat16, jnp.float32
MIB = 1024 * 1024
IN_VMEM = pl.BlockSpec(memory_space=pltpu.VMEM)
IN_SMEM = pl.BlockSpec(memory_space=pltpu.SMEM)
IN_HBM = pl.BlockSpec(memory_space=pltpu.HBM)
ANYWHERE = pl.BlockSpec(memory_space=pl.ANY)
TOKEN = jax.ShapeDtypeStruct((8, 128), F32)


def gelu_parts(hidden_pre):
    normal_cdf = 0.5 * (1.0 + lax.erf(hidden_pre * 0.7071067811865476))
    normal_pdf = jnp.exp(-0.5 * hidden_pre * hidden_pre) * 0.3989422804014327
    return (hidden_pre * normal_cdf, normal_cdf + hidden_pre * normal_pdf)


def dot(left, right, left_dim, right_dim):
    return lax.dot_general(
        left, right, (((left_dim,), (right_dim,)), ((), ())), preferred_element_type=F32
    )


def shape(*sizes, kind=BF16):
    return jax.ShapeDtypeStruct(sizes, kind)


class Chain:
    def __init__(self, where):
        self.where = where
        self.token = jnp.zeros(TOKEN.shape, TOKEN.dtype)

    def __call__(self, kernel, inputs, out_shapes, after=(), scratch=(), limit=16, specs=None, to=IN_VMEM):
        n_in, n_after, n_out = len(inputs), len(after) + 1, len(out_shapes)

        def body(where, *refs):
            ins = refs[:n_in]
            outs = refs[n_in + n_after : n_in + n_after + n_out]
            token = refs[n_in + n_after + n_out]
            kernel(where, ins, outs, refs[n_in + n_after + n_out + 1 :])
            token[...] = jnp.zeros(token.shape, token.dtype)

        *results, self.token = pl.pallas_call(
            body,
            in_specs=[IN_SMEM] + (specs or [IN_VMEM] * n_in) + [ANYWHERE] * n_after,
            out_specs=[to] * n_out + [IN_VMEM],
            out_shape=list(out_shapes) + [TOKEN],
            scratch_shapes=list(scratch),
            compiler_params=pltpu.CompilerParams(vmem_limit_bytes=limit * MIB),
            cost_estimate=pl.CostEstimate(flops=1000, bytes_accessed=1000, transcendentals=0),
        )(self.where, *inputs, *after, self.token)
        return results


def block_of(where, rel, index, width):
    core = where[0] if rel == 0 else 1 - where[0]
    return pl.ds(pl.multiple_of((2 * index + core) * width, 128), width)


def cut_parts(where, chunks, own_part, messages):
    (rows, part), n_depth = own_part.shape, len(messages) + 1
    own_part[...] = chunks[-1][0, :, pl.ds(pl.multiple_of(where[1] * part, 128), part)]
    for k, message in enumerate(messages, 1):
        owner = lax.rem(where[1] + k, n_depth)
        for index, both in enumerate(chunks):
            at = slice(index * rows, (index + 1) * rows)
            message[at, :part] = both[0, :, pl.ds(pl.multiple_of(owner * part, 128), part)]
            message[at, part:] = both[1]


def hidden_kernel(where, ins, outs, scratch):
    both, weight_in, weight_out = ins[:3]
    other_hidden, other_grad, own = outs[:3]
    blocks, _, width = other_hidden.shape
    for rel in (1, 0):
        targets = (own.at[0], own.at[1]) if rel == 0 else (other_hidden, other_grad)
        for index in range(blocks):
            cut = block_of(where, rel, index, width)
            targets[0][index] = dot(both[0], weight_in[:, cut], 1, 0).astype(BF16)
            targets[1][index] = dot(both[1], weight_out[cut, :], 1, 1).astype(BF16)
    cut_parts(where, list(ins[3:]) + [both], outs[3], outs[4:])


def first_kernel(where, ins, outs, scratch):
    both, from_in, from_out = ins
    own, weight_in, weight_out, own_part = outs[:4]
    _, blocks, _, width = own.shape
    n_others = 2 * blocks
    others, messages = outs[-n_others:], outs[4:-n_others]
    steps = []
    for rel in (1, 0):
        for index in range(blocks):
            cut = block_of(where, rel, index, width)
            for which, source, target in ((0, from_in, weight_in), (1, from_out, weight_out)):
                at = (slice(None), cut) if which == 0 else (cut, slice(None))
                copy = pltpu.make_async_copy(source.at[at], target.at[at], scratch[0].at[len(steps)])
                copy.start()
                spot = others[which * blocks + index] if rel else own.at[which].at[index]
                steps.append((copy, which, at, spot))
    cut_parts(where, [both], own_part, messages)
    for copy, which, at, spot in steps:
        copy.wait()
        weight = weight_out if which else weight_in
        spot[...] = dot(both[which], weight[at], 1, which).astype(BF16)


def chip_kernel(where, ins, outs, scratch):
    blocks = ins[0].shape[1]
    for which in range(2):
        for index in range(blocks):
            came = ins[1 + which][index] if len(ins) == 3 else ins[1 + which * blocks + index][...]
            total = ins[0][which, index].astype(F32) + came.astype(F32)
            outs[0][which, index] = total.astype(BF16)


def gelu_kernel(where, ins, outs, scratch):
    blocks = ins[0].shape[1]
    depth, n_depth = where[1], len(outs)
    for index in range(blocks):
        hidden, grad = ins[0][0, index].astype(F32), ins[0][1, index].astype(F32)
        for other in ins[1:]:
            hidden += other[0, index].astype(F32)
            grad += other[1, index].astype(F32)
        value, slope = gelu_parts(hidden)
        act, pre = value.astype(BF16), (grad * slope).astype(BF16)
        outs[0][0, index] = act
        outs[0][1, index] = pre
        for message in outs[1:]:
            message[index] = pre
    for k in range(1, n_depth):
        outs[k][blocks] = outs[0][0, lax.rem(depth + k, n_depth)]


def model_kernel(where, ins, outs, scratch):
    weight_in, weight_out = ins[2:4]
    _, blocks, _, width = ins[0].shape
    out = grad = 0.0
    for rel in range(2):
        for index in range(blocks):
            cut = block_of(where, rel, index, width)
            out += dot(ins[rel][0, index], weight_out[cut, :], 1, 0)
            grad += dot(ins[rel][1, index], weight_in[:, cut], 1, 1)
    if len(ins) > 4:
        out += ins[4][0].astype(F32)
        grad += ins[4][1].astype(F32)
    outs[0][0] = out.astype(BF16)
    outs[0][1] = grad.astype(BF16)


def relay_kernel(where, ins, outs, scratch):
    for index, target in enumerate(outs):
        target[...] = ins[0][index]


def final_kernel(where, ins, outs, scratch):
    for index in range(2):
        total = ins[0][index].astype(F32) + ins[1][index].astype(F32)
        outs[index][...] = total.astype(BF16)


def weight_kernel(own, far, before, send, where, ins, outs, scratch):
    all_tokens, all_cotangents, all_values = scratch[:3]
    width, part = all_values.shape[1], all_tokens.shape[1]
    blocks = outs[0].shape[1] // (2 * width)
    ins = list(ins)
    tokens, cotangents = [], []
    acts, pres = ([], []), ([], [])
    for _ in range(own):
        share, both, *values = (ins.pop(0) for _ in range(4))
        rows = share.shape[0]
        tokens.append(share)
        cotangents.append(both.at[1])
        for rel, value in enumerate(values):
            acts[rel].append(value.at[0].at[where[1]])
            pres[rel].append([value.at[1].at[index] for index in range(blocks)])
    for start in far:
        sent, mine = ins.pop(0), ins.pop(0)
        rows = mine.shape[1]
        tokens.append(sent.at[start : start + rows, :part])
        cotangents.append(sent.at[start : start + rows, part:])
        pieces = [mine.at[index] for index in range(blocks + 1)]
        if send:
            swapped = [ins.pop(0) for _ in range(blocks + 1)]
        else:
            swapped = ins.pop(0)
            swapped = [swapped.at[index] for index in range(blocks + 1)]
        for rel, value in enumerate((pieces, swapped)):
            acts[rel].append(value[blocks])
            pres[rel].append(value[:blocks])

    def fill(target, sources):
        for index, source in enumerate(sources):
            target[index * rows : (index + 1) * rows, :] = source[...]

    copies = []

    def put(which, at, term):
        if before:
            term += ins[which][at]
        if not send:
            outs[which][at] = term
            return
        held, semaphore = scratch[3 + which], scratch[5].at[len(copies)]
        held[at] = term
        copies.append(pltpu.make_async_copy(held.at[at], outs[which].at[at], semaphore))
        copies[-1].start()

    fill(all_tokens, tokens)
    fill(all_cotangents, cotangents)
    for rel in range(2):
        core = where[0] if rel == 0 else 1 - where[0]
        for index in range(blocks):
            fill(all_values, [value[index] for value in pres[rel]])
            at = (slice(None), block_of(where, rel, index, width))
            put(0, at, dot(all_tokens[...], all_values[...], 0, 0))
        fill(all_values, acts[rel])
        at = (pl.ds(pl.multiple_of(core * width, 128), width), slice(None))
        put(1, at, dot(all_values[...], all_cotangents[...], 0, 0))
    for copy in copies:
        copy.wait()


class Plain:
    def __init__(self, core, depth, n_depth):
        self.core, self.depth, self.n_depth = core, depth, n_depth

    def split(self, value, axis):
        size = value.shape[axis] // (2 * self.n_depth)
        lead = value.shape[:axis] + (self.n_depth, 2, size) + value.shape[axis + 1 :]
        value = value.reshape(lead)
        take = lambda c: lax.dynamic_index_in_dim(value, c, axis + 1, False)
        return take(self.core), take(1 - self.core)

    def join(self, own, other):
        first = jnp.where(self.core == 0, own, other)
        second = jnp.where(self.core == 0, other, own)
        return jnp.stack([first, second], axis=-3)

    def hidden(self, both, weight_in, weight_out):
        hidden = dot(both[0], weight_in, 1, 0).astype(BF16)
        grad = dot(both[1], weight_out, 1, 1).astype(BF16)
        pairs = zip(self.split(hidden, 1), self.split(grad, 1))
        own, other = (jnp.stack([h, g]).transpose(0, 2, 1, 3) for h, g in pairs)
        return other, own

    def parts(self, both, size):
        cuts = [
            lax.dynamic_slice_in_dim(both[0], (self.depth + k) % self.n_depth * size, size, 1)
            for k in range(self.n_depth)
        ]
        return cuts[:1] + [jnp.concatenate([cut, both[1]], axis=1) for cut in cuts[1:]]

    def gelu(self, parts):
        total = sum(part.astype(F32) for part in parts)
        value, slope = gelu_parts(total[0])
        act, pre = value.astype(BF16), (total[1] * slope).astype(BF16)
        messages = []
        for k in range(1, self.n_depth):
            share = lax.dynamic_index_in_dim(act, (self.depth + k) % self.n_depth, 0)
            messages.append(jnp.concatenate([pre, share]))
        return [jnp.stack([act, pre])] + messages

    def flat(self, own, other):
        joined = self.join(own, other)
        blocks, cores, rows, width = joined.shape
        return joined.transpose(2, 0, 1, 3).reshape(rows, blocks * cores * width)

    def model(self, own, other, weight_in, weight_out, arrived):
        out = dot(self.flat(own[0], other[0]), weight_out, 1, 0)
        grad = dot(self.flat(own[1], other[1]), weight_in, 1, 1)
        sums = jnp.stack([out, grad])
        return (sums + sum(value.astype(F32) for value in arrived)).astype(BF16)

    def weights(self, own_rows, far_rows):
        in_grad = out_grad = 0.0
        for part, both, own, other in own_rows:
            act = [lax.dynamic_index_in_dim(v[0], self.depth, 0) for v in (own, other)]
            in_grad += dot(part, self.flat(own[1], other[1]), 0, 0)
            out_grad += dot(self.flat(*act), both[1], 0, 0)
        for (sent, own, other), start in far_rows:
            sent = sent[start : start + own.shape[1]]
            size = sent.shape[1] - own_rows[0][1].shape[2]
            part, cotangent = sent[:, :size], sent[:, size:]
            in_grad += dot(part, self.flat(own[:-1], other[:-1]), 0, 0)
            out_grad += dot(self.flat(own[-1:], other[-1:]), cotangent, 0, 0)
        return in_grad, out_grad


def shards(n_row, n_col, n_depth, tokens, weight_in, weight_out, output_grad):
    core = lax.axis_index("row") % 2
    depth = lax.axis_index("depth")
    rows, features = tokens.shape
    part = features // n_depth
    blocks, width = n_depth, weight_in.shape[1] // (2 * n_depth)
    aligned = width % 128 == 0 and part % 128 == 0
    chain = Chain(jnp.stack([core, depth]).astype(jnp.int32))
    plain = Plain(core, depth, n_depth)

    def swap_cores(value):
        return lax.ppermute(value, "row", [(r, r ^ 1) for r in range(n_row)])

    def to_chip(value, k):
        return lax.ppermute(value, "row", [(r, (r + 2 * k) % n_row) for r in range(n_row)])

    def to_depth(value, k):
        return lax.ppermute(value, "depth", [(d, (d + k) % n_depth) for d in range(n_depth)])

    def to_next(value):
        return lax.ppermute(value, "col", [(c, (c + 1) % n_col) for c in range(n_col)])

    far = range(1, n_depth)
    pair_shape = shape(2, blocks, rows, width)
    both = [jnp.stack([tokens, output_grad])]
    chips, crossed, parts, far_parts = {}, {}, {}, {}

    weights = [weight_in, weight_out]
    pairs, swaps = {}, {}
    late = []
    n_single = min(2, n_col - 1)

    def place(stage):
        return max(stage - n_single, 0) * rows

    def hidden_step(stage):
        single = shape(blocks, rows, width)
        if stage < n_single:
            waiting = []
        else:
            waiting = both[n_single:stage] if stage == n_col - 1 else None
        cuts = [shape(rows, part)]
        if waiting is not None:
            cuts += [shape(rows * (len(waiting) + 1), part + features)] * (n_depth - 1)
        if not aligned:
            others, own = plain.hidden(both[stage], *weights)
            parts[stage], *sent = plain.parts(both[stage], part)
            if stage >= n_single:
                late.append(sent)
                sent = [jnp.concatenate(values) for values in zip(*late)]
        elif stage == 0:
            results = chain(
                first_kernel,
                [both[stage]] + weights,
                [pair_shape, shape(*weight_in.shape), shape(*weight_out.shape)]
                + cuts
                + [shape(rows, width)] * (2 * blocks),
                scratch=[pltpu.SemaphoreType.DMA((4 * blocks,))],
                specs=[IN_VMEM, IN_HBM, IN_HBM],
                limit=42,
            )
            own, weights[0], weights[1], parts[stage] = results[:4]
            sent, others = results[4 : -2 * blocks], results[-2 * blocks :]
        else:
            results = chain(
                hidden_kernel,
                [both[stage]] + weights + (waiting or []),
                [single, single, pair_shape] + cuts,
                after=far_parts[0] if stage == 1 else [],
            )
            *others, own, parts[stage] = results[:4]
            sent = results[4:]
        if stage + 1 < n_col:
            both.append(to_next(both[stage]))
        came = [swap_cores(other) for other in others]
        if aligned:
            (chips[stage],) = chain(chip_kernel, [own] + came, [pair_shape])
        else:
            chips[stage] = (own.astype(F32) + jnp.stack(came).astype(F32)).astype(BF16)
        crossed[stage] = [to_chip(chips[stage], k) for k in range(1, n_row // 2)]
        if waiting is not None:
            far_parts[stage] = [to_depth(sent[k - 1], k) for k in far]

    own_rows, far_came = [], []

    def gelu_step(stage):
        if aligned:
            after = {0: far_parts.get(1, []), n_col - 2: far_parts.get(n_col - 1, [])}.get(stage, [])
            after = list(after)
            if stage > 0:
                after += far_came[stage - 1]
            pairs[stage], *messages = chain(
                gelu_kernel,
                [chips[stage]] + crossed[stage],
                [pair_shape] + [shape(blocks + 1, rows, width)] * (n_depth - 1),
                after=after,
            )
        else:
            pairs[stage], *messages = plain.gelu([chips[stage]] + crossed[stage])
        swaps[stage] = swap_cores(pairs[stage])
        own_rows.append([parts[stage], both[stage], pairs[stage], swaps[stage]])
        group = []
        for k in far:
            group.append(to_depth(messages[k - 1], k))
        far_came.append(group)

    kept, arrived = None, []

    def model_step(stage):
        nonlocal kept, arrived
        if aligned:
            (sums,) = chain(
                model_kernel,
                [pairs[stage], swaps[stage]] + weights + arrived,
                [shape(2, rows, features)],
            )
        else:
            sums = plain.model(pairs[stage], swaps[stage], *weights, arrived)
        if stage == 0:
            kept = sums
        else:
            arrived = [to_next(sums)]

    for stage in range(n_col):
        hidden_step(stage)
        if stage > 1:
            model_step(stage - 2)
        if stage > 0:
            gelu_step(stage - 1)
    model_step(n_col - 2)
    gelu_step(n_col - 1)
    model_step(n_col - 1)

    far_rows = [
        [
            [far_parts[stage if stage < n_single else n_col - 1][k - 1], far_came[stage][k - 1]]
            for k in far
        ]
        for stage in range(n_col)
    ]
    groups = [(row, stage) for stage, group in enumerate(far_rows[:-1]) for row in group]
    early_rows = [(row + [swap_cores(row[1])], place(stage)) for row, stage in groups]
    if aligned:
        grads = [
            shape(part, 2 * blocks * width, kind=F32),
            shape(2 * width, features, kind=F32),
        ]

        def weight_call(own, away, before, send):
            count = rows * (len(own) + len(away))
            starts = [start for _, start in away]
            scratch = [
                pltpu.VMEM((count, part), BF16),
                pltpu.VMEM((count, features), BF16),
                pltpu.VMEM((count, width), BF16),
            ]
            if send:
                scratch += [pltpu.VMEM(grad.shape, F32) for grad in grads]
                scratch += [pltpu.SemaphoreType.DMA((2 * blocks + 2,))]
            values = [value for row in own for value in row]
            values += [value for row, _ in away for value in row]
            return chain(
                functools.partial(weight_kernel, len(own), starts, bool(before), send),
                values + list(before),
                grads,
                scratch=scratch,
                limit=24,
                to=IN_HBM if send else IN_VMEM,
            )

        terms = weight_call(own_rows, early_rows, (), not far)
        if far:
            last_rows = []
            for sent, came in far_rows[-1]:
                pieces = chain(relay_kernel, [came], [shape(rows, width)] * (blocks + 1))
                swapped = [swap_cores(piece) for piece in pieces]
                last_rows.append(([sent, came] + swapped, place(n_col - 1)))
            terms = weight_call((), last_rows, terms, True)
        output, input_grad = chain(
            final_kernel, [kept] + arrived, [shape(rows, features)] * 2
        )
    else:
        last_rows = [(row + [swap_cores(row[1])], place(n_col - 1)) for row in far_rows[-1]]
        terms = plain.weights(own_rows, early_rows + last_rows)
        output, input_grad = (kept.astype(F32) + arrived[0].astype(F32)).astype(BF16)
    return (output, input_grad, *terms)


def solution(mesh):
    placed = (
        P(("col", "depth"), "row"),
        P("row", "col"),
        P("col", "row"),
        P(("col", "depth"), "row"),
    )
    sizes = (mesh.shape["row"], mesh.shape["col"], mesh.shape["depth"])
    return jax.shard_map(
        functools.partial(shards, *sizes),
        mesh=mesh,
        in_specs=placed,
        out_specs=(
            P(("col", "depth"), "row"),
            P(("col", "depth"), "row"),
            P(("row", "depth"), "col"),
            P(("col", "depth"), "row"),
        ),
        check_vma=False,
    )
```

```python
import functools

import jax
import jax.numpy as jnp
from jax import lax
from jax.experimental import pallas as pl
from jax.experimental.pallas import tpu as pltpu
from jax.sharding import PartitionSpec as P

BF16, F32 = jnp.bfloat16, jnp.float32
MIB = 1024 * 1024
IN_VMEM = pl.BlockSpec(memory_space=pltpu.VMEM)
IN_SMEM = pl.BlockSpec(memory_space=pltpu.SMEM)
IN_HBM = pl.BlockSpec(memory_space=pltpu.HBM)
ANYWHERE = pl.BlockSpec(memory_space=pl.ANY)
TOKEN = jax.ShapeDtypeStruct((8, 128), F32)


def gelu_parts(hidden_pre):
    normal_cdf = 0.5 * (1.0 + lax.erf(hidden_pre * 0.7071067811865476))
    normal_pdf = jnp.exp(-0.5 * hidden_pre * hidden_pre) * 0.3989422804014327
    return (hidden_pre * normal_cdf, normal_cdf + hidden_pre * normal_pdf)


def dot(left, right, left_dim, right_dim):
    return lax.dot_general(
        left, right, (((left_dim,), (right_dim,)), ((), ())), preferred_element_type=F32
    )


def shape(*sizes, kind=BF16):
    return jax.ShapeDtypeStruct(sizes, kind)


class Chain:
    def __init__(self, where):
        self.where = where
        self.token = jnp.zeros(TOKEN.shape, TOKEN.dtype)

    def __call__(
        self, kernel, inputs, out_shapes, after=(), scratch=(), limit=16, specs=None, to=IN_VMEM
    ):
        n_in, n_after, n_out = len(inputs), len(after) + 1, len(out_shapes)

        def body(where, *refs):
            ins = refs[:n_in]
            outs = refs[n_in + n_after : n_in + n_after + n_out]
            token = refs[n_in + n_after + n_out]
            kernel(where, ins, outs, refs[n_in + n_after + n_out + 1 :])
            token[...] = jnp.zeros(token.shape, token.dtype)

        *results, self.token = pl.pallas_call(
            body,
            in_specs=[IN_SMEM] + (specs or [IN_VMEM] * n_in) + [ANYWHERE] * n_after,
            out_specs=[to] * n_out + [IN_VMEM],
            out_shape=list(out_shapes) + [TOKEN],
            scratch_shapes=list(scratch),
            compiler_params=pltpu.CompilerParams(vmem_limit_bytes=limit * MIB),
            cost_estimate=pl.CostEstimate(flops=1000, bytes_accessed=1000, transcendentals=0),
        )(self.where, *inputs, *after, self.token)
        return results


def block_of(where, rel, index, width):
    core = where[0] if rel == 0 else 1 - where[0]
    return pl.ds(pl.multiple_of((2 * index + core) * width, 128), width)


def part_of(where, owner, part):
    return pl.ds(pl.multiple_of(owner * part, 128), part)


def cut_shares(where, both, features, messages):
    for k, message in enumerate(messages, 1):
        part = message.shape[1] - features
        owner = lax.rem(where[1] + k, len(messages) + 1)
        message[:, :part] = both[:, part_of(where, owner, part)]
        message[:, part:] = both[:, features : 2 * features]


def fetch(where, rel, sources, targets, semaphores):
    from_in, from_out = sources
    weight_in, weight_out = targets
    copies = []
    for index in range(weight_in.shape[0]):
        cut = block_of(where, rel, index, weight_in.shape[2])
        for source, target in (
            (from_in.at[:, cut], weight_in.at[index]),
            (from_out.at[cut, :], weight_out.at[index]),
        ):
            copies.append(pltpu.make_async_copy(source, target, semaphores.at[len(copies)]))
            copies[-1].start()
    return copies


def fetch_kernel(where, ins, outs, scratch):
    copies = fetch(where, 1, ins[2:], outs[1:3], scratch[0])
    features = ins[0].shape[1]
    outs[0][:, :features] = ins[0][...]
    outs[0][:, features:] = ins[1][...]
    cut_shares(where, outs[0], features, outs[3:])
    for copy in copies:
        copy.wait()


def other_kernel(where, ins, outs, scratch):
    both, weight_in, weight_out = ins
    features = weight_in.shape[1]
    for index in range(weight_in.shape[0]):
        outs[0][index] = dot(both[:, :features], weight_in[index], 1, 0).astype(BF16)
        outs[1][index] = dot(both[:, features:], weight_out[index], 1, 1).astype(BF16)


def own_kernel(where, ins, outs, scratch):
    both, *sources = ins
    weight_in, weight_out, hidden, grad = outs
    copies = fetch(where, 0, sources, outs[:2], scratch[0])
    features = weight_in.shape[1]
    for index in range(weight_in.shape[0]):
        copies[2 * index].wait()
        hidden[index] = dot(both[:, :features], weight_in[index], 1, 0).astype(BF16)
        copies[2 * index + 1].wait()
        grad[index] = dot(both[:, features:], weight_out[index], 1, 1).astype(BF16)


def arrive_kernel(where, ins, outs, scratch):
    outs[0][...] = ins[0][...]
    for number, value in enumerate(ins[1:]):
        rows = value.shape[0]
        outs[1][number * rows : (number + 1) * rows, :] = value[...]


def join_kernel(where, ins, outs, scratch):
    for which in range(2):
        total = ins[which][...].astype(F32) + ins[2 + which][...].astype(F32)
        outs[0][which] = total.astype(BF16)


def hidden_kernel(keep, where, ins, outs, scratch):
    own, other, own_in, own_out, other_in, other_out = ins
    if keep:
        outs[-2][...] = other_in[...]
        outs[-1][...] = other_out[...]
    cut_shares(where, own, own_in.shape[1], outs[1 : len(outs) - 2 * keep])
    features = own_in.shape[1]
    tokens, cotangents = slice(0, features), slice(features, 2 * features)
    for index in range(own_in.shape[0]):
        hidden = dot(own[:, tokens], own_in[index], 1, 0)
        hidden += dot(other[:, tokens], other_in[index], 1, 0)
        outs[0][0, index] = hidden.astype(BF16)
        grad = dot(own[:, cotangents], own_out[index], 1, 1)
        grad += dot(other[:, cotangents], other_out[index], 1, 1)
        outs[0][1, index] = grad.astype(BF16)


def gelu_kernel(n_depth, where, ins, outs, scratch):
    blocks = ins[0].shape[1]
    depth = where[1]
    n_late = (n_depth - 1) * (len(outs) - n_depth)
    ins, late = ins[: len(ins) - n_late], ins[len(ins) - n_late :]
    for index in range(blocks):
        hidden, grad = ins[0][0, index].astype(F32), ins[0][1, index].astype(F32)
        for other in ins[1:]:
            hidden += other[0, index].astype(F32)
            grad += other[1, index].astype(F32)
        value, slope = gelu_parts(hidden)
        act, pre = value.astype(BF16), (grad * slope).astype(BF16)
        outs[0][0, index] = act
        outs[0][1, index] = pre
        for message in outs[1:]:
            message[index] = pre
    for k in range(1, n_depth):
        outs[k][blocks] = outs[0][0, lax.rem(depth + k, n_depth)]
    for message in outs[n_depth:]:
        message[blocks] = outs[0][0, depth]
        for number, value in enumerate(late, 1):
            message[number * (blocks + 1) : (number + 1) * (blocks + 1)] = value[...]


def model_kernel(where, ins, outs, scratch):
    pair, *weights = ins
    for rel, target in enumerate(outs):
        weight_in, weight_out = weights[2 * rel : 2 * rel + 2]
        out = grad = 0.0
        for index in range(pair.shape[1]):
            out += dot(pair[0, index], weight_out[index], 1, 0)
            grad += dot(pair[1, index], weight_in[index], 1, 1)
        target[0] = out.astype(BF16)
        target[1] = grad.astype(BF16)


def sum_kernel(where, ins, outs, scratch):
    for index in range(2):
        total = sum(value[index].astype(F32) for value in ins)
        if len(outs) == 1:
            outs[0][index] = total.astype(BF16)
        else:
            outs[index][...] = total.astype(BF16)


def early_kernel(near, where, ins, outs, scratch):
    all_tokens, all_cotangents, all_values = scratch
    own_in, own_out, other_in, other_out = outs
    blocks, part, width = own_in.shape
    features = own_out.shape[1]
    pairs, shares, came = ins[2 * near : 3 * near], ins[3 * near : 3 * near + 2], ins[3 * near + 2 :]
    rows = ins[0].shape[0]
    for rel in range(2):
        here = slice(rel * part, (rel + 1) * part)
        there = slice(rel * features, (rel + 1) * features)
        for number in range(near):
            at, source = slice(number * rows, (number + 1) * rows), ins[rel * near + number]
            all_tokens[at, here] = source[:, part_of(where, where[1], part)]
            all_cotangents[at, there] = source[:, features : 2 * features]
        for number in range(len(came)):
            at, source = slice(number * rows, (number + 1) * rows), shares[rel]
            start = (near + number) * rows
            all_tokens[start : start + rows, here] = source[at, :part]
            all_cotangents[start : start + rows, there] = source[at, part:]
    acts = [pair.at[0].at[where[1]] for pair in pairs] + [value.at[blocks] for value in came]
    pres = [[pair.at[1].at[index] for index in range(blocks)] for pair in pairs]
    pres += [[value.at[index] for index in range(blocks)] for value in came]

    def fill(sources):
        for number, source in enumerate(sources):
            all_values[number * rows : (number + 1) * rows, :] = source[...]

    for index in range(blocks):
        fill([value[index] for value in pres])
        term = dot(all_tokens[...], all_values[...], 0, 0)
        own_in[index] = term[:part]
        other_in[index] = term[part:].astype(BF16)
    fill(acts)
    term = dot(all_values[...], all_cotangents[...], 0, 0)
    own_out[...] = term[:, :features]
    other_out[...] = term[:, features:].astype(BF16)


def relay_kernel(where, ins, outs, scratch):
    outs[0][...] = ins[0][...]


def last_kernel(groups, where, ins, outs, scratch):
    all_tokens, all_cotangents, all_values, held_in, held_out, semaphores = scratch
    own, pair, late, *ins = ins
    early = ins[-4:]
    shares, ins = ins[: 2 * groups], ins[2 * groups :]
    _, blocks, rows, width = pair.shape
    part, features = all_tokens.shape[1], all_cotangents.shape[1]
    before, came, swapped = ins[:groups], ins[groups : 2 * groups], ins[2 * groups : 3 * groups]
    values = ([[pair.at[1].at[index] for index in range(blocks)]], [])
    values[0][0].append(pair.at[0].at[where[1]])
    for number in range(groups + 1):
        start = number * (blocks + 1)
        values[1].append([late.at[start + index] for index in range(blocks + 1)])
    for value in list(before) + list(came):
        values[0].append([value.at[index] for index in range(blocks + 1)])
    for value in swapped:
        values[1].append([value.at[index] for index in range(blocks + 1)])
    all_tokens[:rows, :] = own[:, part_of(where, where[1], part)]
    all_cotangents[:rows, :] = own[:, features : 2 * features]
    for number in range(2 * groups):
        start = (number + 1) * rows
        all_tokens[start : start + rows, :] = shares[number][:, :part]
        all_cotangents[start : start + rows, :] = shares[number][:, part:]
    copies = []

    def fill(sources):
        for number, source in enumerate(sources):
            all_values[number * rows : (number + 1) * rows, :] = source[...]

    def put(held, target, at, term):
        held[at] = term
        copies.append(pltpu.make_async_copy(held.at[at], target.at[at], semaphores.at[len(copies)]))
        copies[-1].start()

    for rel in range(2):
        early_in, early_out = early[2 * rel : 2 * rel + 2]
        core = where[0] if rel == 0 else 1 - where[0]
        for index in range(blocks):
            fill([value[index] for value in values[rel]])
            term = dot(all_tokens[...], all_values[...], 0, 0) + early_in[index].astype(F32)
            put(held_in, outs[0], (slice(None), block_of(where, rel, index, width)), term)
        fill([value[blocks] for value in values[rel]])
        term = dot(all_values[...], all_cotangents[...], 0, 0) + early_out[...].astype(F32)
        at = (pl.ds(pl.multiple_of(core * width, 128), width), slice(None))
        put(held_out, outs[1], at, term)
    for copy in copies:
        copy.wait()


def shards(n_row, n_col, n_depth, tokens, weight_in, weight_out, output_grad):
    rows, features = tokens.shape
    part = features // n_depth
    blocks, width = n_depth, weight_in.shape[1] // (2 * n_depth)
    core = lax.axis_index("row") % 2
    depth = lax.axis_index("depth")
    chain = Chain(jnp.stack([core, depth]).astype(jnp.int32))

    def swap_cores(value):
        return lax.ppermute(value, "row", [(r, r ^ 1) for r in range(n_row)])

    def to_chip(value, k):
        return lax.ppermute(value, "row", [(r, (r + 2 * k) % n_row) for r in range(n_row)])

    def to_depth(value, k):
        return lax.ppermute(value, "depth", [(d, (d + k) % n_depth) for d in range(n_depth)])

    def to_col(value, k):
        return lax.ppermute(value, "col", [(c, (c + k) % n_col) for c in range(n_col)])

    single, pair_shape = shape(blocks, rows, width), shape(2, blocks, rows, width)
    model_shape = shape(2, rows, features)
    message_shape = shape(blocks + 1, rows, width)
    weight_shapes = [shape(blocks, features, width), shape(blocks, width, features)]
    groups = n_depth - 1
    last = n_col - 1
    own, other, shares = {}, {}, {}
    chip, crossed, pairs, came, model = {}, {}, {}, {}, {}

    def cross(stage):
        crossed[stage] = [to_chip(chip[stage], k) for k in range(1, n_row // 2)]

    share_shapes = [shape(rows, part + features)] * groups
    semaphores = [pltpu.SemaphoreType.DMA((2 * blocks,))]

    def send_shares(stage, values):
        shares[stage] = [to_depth(value, k) for k, value in enumerate(values, 1)]

    own[0], sent_in, sent_out, *results = chain(
        fetch_kernel,
        [tokens, output_grad, weight_in, weight_out],
        [shape(rows, 2 * features)] + weight_shapes + share_shapes,
        scratch=semaphores,
        specs=[IN_VMEM, IN_VMEM, IN_HBM, IN_HBM],
        limit=48,
    )
    send_shares(0, results)
    other_weights = [swap_cores(sent_in), swap_cores(sent_out)]
    results = chain(other_kernel, [own[0], sent_in, sent_out], [single, single])
    swapped = [swap_cores(value) for value in results]
    *own_weights, hidden, grad = chain(
        own_kernel,
        [own[0], weight_in, weight_out],
        weight_shapes + [single, single],
        scratch=semaphores,
        specs=[IN_VMEM, IN_HBM, IN_HBM],
        limit=44,
    )
    (chip[0],) = chain(join_kernel, [hidden, grad] + swapped, [pair_shape])
    cross(0)
    other[0] = swap_cores(own[0])
    own[1] = to_col(own[0], 1)
    raw, early_shares = {1: own[1]}, []

    def arrive_step(stage, after=()):
        raw[stage] = to_col(raw[stage - 1], 1)
        near, stacked = [raw[stage]], []
        if stage == last - 1:
            near += [value for earlier in range(stage) for value in shares[earlier]]
            stacked = [shape(stage * groups * rows, part + features)]
        own[stage], *results = chain(
            arrive_kernel, near, [shape(rows, 2 * features)] + stacked, after=after
        )
        if results:
            early_shares.extend(results + [swap_cores(results[0])])

    def hidden_step(stage, after=()):
        other[stage] = swap_cores(own[stage])
        chip[stage], *results = chain(
            functools.partial(hidden_kernel, stage == 1),
            [own[stage], other[stage]] + own_weights + other_weights,
            [pair_shape] + share_shapes + (weight_shapes if stage == 1 else []),
            after=after,
        )
        send_shares(stage, results[:groups])
        other_weights[:] = results[groups:] or other_weights
        cross(stage)

    def gelu_step(stage, after=()):
        inputs, outputs = [chip[stage]] + crossed[stage], [pair_shape] + [message_shape] * groups
        if stage == last:
            inputs += came[stage - 1]
            outputs += [shape(n_depth * (blocks + 1), rows, width)]
        pairs[stage], *messages = chain(
            functools.partial(gelu_kernel, n_depth), inputs, outputs, after=after
        )
        came[stage] = [to_depth(value, k) for k, value in enumerate(messages[:groups], 1)]
        return messages[groups:]

    def model_step(stage, after=()):
        mine, theirs = chain(
            model_kernel, [pairs[stage]] + own_weights + other_weights, [model_shape] * 2, after=after
        )
        model[stage] = [mine, swap_cores(theirs)]

    def sum_step(stage):
        arrived = ring[stage - 1] if stage > 1 else []
        (total,) = chain(sum_kernel, model[stage] + arrived, [model_shape])
        ring[stage] = [to_col(total, 1)]

    ring = {}
    hidden_step(1, shares[0])
    gelu_step(0, [other[0]])
    for stage in range(2, n_col):
        arrive_step(stage, shares[stage - 1])
        model_step(stage - 2)
        hidden_step(stage)
        after = came[stage - 2] + (model[0] if stage == 2 else [])
        gelu_step(stage - 1, after)
        if stage > 2:
            sum_step(stage - 2)
    model_step(last - 1)
    near = list(range(last))
    early_values = [values[stage] for values in (own, other, pairs) for stage in near]
    early_values += early_shares
    early_values += [value for stage in range(last - 1) for value in came[stage]]
    count = rows * (last + (last - 1) * groups)
    term_sizes = [(blocks, part, width), (width, features)]
    *own_early, sent_in, sent_out = chain(
        functools.partial(early_kernel, last),
        early_values,
        [shape(*share, kind=kind) for kind in (F32, BF16) for share in term_sizes],
        scratch=[
            pltpu.VMEM((count, 2 * part), BF16),
            pltpu.VMEM((count, 2 * features), BF16),
            pltpu.VMEM((count, width), BF16),
        ],
        limit=24,
    )
    other_early = [swap_cores(sent_in), swap_cores(sent_out)]
    (late,) = gelu_step(last, shares[last])
    late = swap_cores(late)
    model_step(last)
    sum_step(last - 1)
    sum_step(last)
    relayed = [
        value
        for source in came[last]
        for value in chain(relay_kernel, [source], [message_shape])
    ]
    last_values = [own[last], pairs[last], late] + shares[last - 1] + shares[last]
    last_values += came[last - 1] + came[last]
    last_values += [swap_cores(value) for value in relayed]
    count = rows * (1 + 2 * groups)
    grads = [shape(part, 2 * blocks * width, kind=F32), shape(2 * width, features, kind=F32)]
    in_grad, out_grad = chain(
        functools.partial(last_kernel, groups),
        last_values + own_early + other_early,
        grads,
        scratch=[
            pltpu.VMEM((count, part), BF16),
            pltpu.VMEM((count, features), BF16),
            pltpu.VMEM((count, width), BF16),
            pltpu.VMEM(grads[0].shape, F32),
            pltpu.VMEM(grads[1].shape, F32),
            pltpu.SemaphoreType.DMA((2 * blocks + 2,)),
        ],
        limit=20,
        to=IN_HBM,
    )
    output, input_grad = chain(
        sum_kernel,
        model[0] + ring[last],
        [shape(rows, features)] * 2,
    )
    return output, input_grad, in_grad, out_grad


def plain_shards(tokens, weight_in, weight_out, output_grad):
    x_panel = lax.all_gather(tokens, "col", axis=0, tiled=True)
    dy_panel = lax.all_gather(output_grad, "col", axis=0, tiled=True)

    def hidden_total(term):
        return lax.psum(term.astype(BF16), "row").astype(F32)

    def scattered(term, axis):
        return lax.psum_scatter(term.astype(BF16), axis, scatter_dimension=0, tiled=True)

    value, slope = gelu_parts(hidden_total(dot(x_panel, weight_in, 1, 0)))
    act = value.astype(BF16)
    pre = (hidden_total(dot(dy_panel, weight_out, 1, 1)) * slope).astype(BF16)
    return (
        scattered(dot(act, weight_out, 1, 0), "col"),
        scattered(dot(pre, weight_in, 1, 1), "col"),
        scattered(dot(x_panel, pre, 0, 0), "depth").astype(F32),
        scattered(dot(act, dy_panel, 0, 0), "depth").astype(F32),
    )


def solution(mesh):
    placed = (
        P(("col", "depth"), "row"),
        P("row", "col"),
        P("col", "row"),
        P(("col", "depth"), "row"),
    )
    sizes = (mesh.shape["row"], mesh.shape["col"], mesh.shape["depth"])

    def local(tokens, weight_in, weight_out, output_grad):
        arrays = (tokens, weight_in, weight_out, output_grad)
        n_row, n_col, n_depth = sizes
        width, part = weight_in.shape[1] // (2 * n_depth), tokens.shape[1] // n_depth
        fits = width % 128 == 0 and part % 128 == 0 and tokens.shape[0] % 16 == 0
        if fits and n_row % 2 == 0 and n_col > 2 and n_depth > 1:
            return shards(*sizes, *arrays)
        return plain_shards(*arrays)

    return jax.shard_map(
        local,
        mesh=mesh,
        in_specs=placed,
        out_specs=(
            P(("col", "depth"), "row"),
            P(("col", "depth"), "row"),
            P(("row", "depth"), "col"),
            P(("col", "depth"), "row"),
        ),
        check_vma=False,
    )
```

```python
import functools

import jax
import jax.numpy as jnp
from jax import lax
from jax.experimental import pallas as pl
from jax.experimental.pallas import tpu as pltpu
from jax.sharding import PartitionSpec as P

BF16, F32 = jnp.bfloat16, jnp.float32
MIB = 1024 * 1024
IN_VMEM = pl.BlockSpec(memory_space=pltpu.VMEM)
IN_SMEM = pl.BlockSpec(memory_space=pltpu.SMEM)
IN_HBM = pl.BlockSpec(memory_space=pltpu.HBM)
ANYWHERE = pl.BlockSpec(memory_space=pl.ANY)
TOKEN = jax.ShapeDtypeStruct((8, 128), F32)


RING = True
HOPS = 0
HALVES = 2
COSTS = {}
PLANS = {
    3: (
        (
            ("H", 1), ("G", 0), ("U", 2), ("M", 0), ("H", 2), ("G", 1),
            ("U", 3), ("M", 1), ("H", 3), ("G", 2), ("S", 1), ("M", 2),
            ("E", 0), ("G", 3), ("G", 4), ("C", 0), ("M", 3), ("S", 2),
            ("S", 3), ("L", 0), ("L", 1), ("F", 0),
        ),
        {
            ("H", 1): (("T", 0),),
            ("G", 0): (("O", 0),),
            ("U", 2): (("T", 1),),
            ("U", 3): (("T", 2),),
            ("G", 1): (("Y", 0), ("M", 0),),
            ("G", 2): (("Y", 1),),
            ("G", 3): (("T", 3),),
        },
    ),
}


def default_plan(last):
    order = [("H", 1), ("G", 0)]
    for stage in range(2, last + 1):
        order += [("U", stage), ("M", stage - 2), ("H", stage), ("G", stage - 1)]
        order += [("S", stage - 2)] if stage > 2 else []
    order += [("M", last - 1), ("E", 0), ("C", 0)]
    order += [("G", last + half) for half in range(HALVES)]
    order += [("M", last), ("S", last - 1), ("S", last)]
    return order + [("L", 0), ("L", 1), ("F", 0)], {}


def gelu_parts(hidden_pre):
    normal_cdf = 0.5 * (1.0 + lax.erf(hidden_pre * 0.7071067811865476))
    normal_pdf = jnp.exp(-0.5 * hidden_pre * hidden_pre) * 0.3989422804014327
    return (hidden_pre * normal_cdf, normal_cdf + hidden_pre * normal_pdf)


def dot(left, right, left_dim, right_dim):
    return lax.dot_general(
        left, right, (((left_dim,), (right_dim,)), ((), ())), preferred_element_type=F32
    )


def shape(*sizes, kind=BF16):
    return jax.ShapeDtypeStruct(sizes, kind)


class Chain:
    def __init__(self, where):
        self.where = where
        self.token = jnp.zeros(TOKEN.shape, TOKEN.dtype)
        self.flops = 1000

    def __call__(
        self,
        kernel,
        inputs,
        out_shapes,
        after=(),
        scratch=(),
        limit=16,
        specs=None,
        to=IN_VMEM,
        filled=0,
    ):
        n_in, n_after, n_out = len(inputs), len(after) + 1, len(out_shapes)

        def body(where, *refs):
            ins = refs[:n_in]
            outs = refs[n_in + n_after : n_in + n_after + n_out]
            token = refs[n_in + n_after + n_out]
            kernel(where, ins, outs, refs[n_in + n_after + n_out + 1 :])
            token[...] = jnp.zeros(token.shape, token.dtype)

        *results, self.token = pl.pallas_call(
            body,
            in_specs=[IN_SMEM] + (specs or [IN_VMEM] * n_in) + [ANYWHERE] * n_after,
            out_specs=[to] * n_out + [IN_VMEM],
            out_shape=list(out_shapes) + [TOKEN],
            scratch_shapes=list(scratch),
            input_output_aliases={1 + n_in - filled + k: k for k in range(filled)},
            compiler_params=pltpu.CompilerParams(vmem_limit_bytes=limit * MIB),
            cost_estimate=pl.CostEstimate(
                flops=self.flops, bytes_accessed=1000, transcendentals=0
            ),
        )(self.where, *inputs, *after, self.token)
        return results


def block_of(where, rel, index, width):
    core = where[0] if rel == 0 else 1 - where[0]
    return pl.ds(pl.multiple_of((2 * index + core) * width, 128), width)


def part_of(where, owner, part):
    return pl.ds(pl.multiple_of(owner * part, 128), part)


def cut_shares(where, both, features, messages):
    for k, message in enumerate(messages, 1):
        part = message.shape[1] - features
        owner = lax.rem(where[1] + k, len(messages) + 1)
        message[:, :part] = both[:, part_of(where, owner, part)]
        message[:, part:] = both[:, features : 2 * features]


def fetch(where, rel, sources, targets, semaphores):
    from_in, from_out = sources
    weight_in, weight_out = targets
    copies = []
    for index in range(weight_in.shape[0]):
        cut = block_of(where, rel, index, weight_in.shape[2])
        for source, target in (
            (from_in.at[:, cut], weight_in.at[index]),
            (from_out.at[cut, :], weight_out.at[index]),
        ):
            copies.append(pltpu.make_async_copy(source, target, semaphores.at[len(copies)]))
            copies[-1].start()
    return copies


def fetch_kernel(where, ins, outs, scratch):
    for copy in fetch(where, 1, ins, outs, scratch[0]):
        copy.wait()


def other_kernel(where, ins, outs, scratch):
    *chunk, weight_in, weight_out = ins
    hidden, grad, both, *messages = outs
    features = weight_in.shape[1]
    both[:, :features] = chunk[0][...]
    both[:, features:] = chunk[1][...]
    cut_shares(where, both, features, messages)
    for index in range(weight_in.shape[0]):
        hidden[index] = dot(chunk[0][...], weight_in[index], 1, 0).astype(BF16)
        grad[index] = dot(chunk[1][...], weight_out[index], 1, 1).astype(BF16)


def own_kernel(where, ins, outs, scratch):
    both, *sources = ins
    copies = fetch(where, 0, sources, outs[:2], scratch[0])
    features = outs[0].shape[1]
    for index in range(outs[0].shape[0]):
        for which in range(2):
            copies[2 * index + which].wait()
            left = both[:, which * features : (which + 1) * features]
            outs[2 + which][index] = dot(left, outs[which][index], 1, which).astype(BF16)


def join_kernel(where, ins, outs, scratch):
    for which in range(2):
        total = ins[which][...].astype(F32) + ins[2 + which][...].astype(F32)
        outs[0][which] = total.astype(BF16)


def arrive_kernel(where, ins, outs, scratch):
    outs[0][...] = ins[0][...]
    for number, value in enumerate(ins[1:]):
        rows = value.shape[0]
        outs[1][number * rows : (number + 1) * rows, :] = value[...]


def lay(targets, which, index, value):
    rows = targets[0].shape[2]
    for number, target in enumerate(targets):
        target[which, index] = value[number * rows : (number + 1) * rows]


def hidden_kernel(keep, pieces, where, ins, outs, scratch):
    own, other, own_in, own_out, other_in, other_out = ins
    if keep:
        outs[-2][...] = other_in[...]
        outs[-1][...] = other_out[...]
    cut_shares(where, own, own_in.shape[1], outs[pieces : len(outs) - 2 * keep])
    features = own_in.shape[1]
    tokens, cotangents = slice(0, features), slice(features, 2 * features)
    for index in range(own_in.shape[0]):
        hidden = dot(own[:, tokens], own_in[index], 1, 0)
        hidden += dot(other[:, tokens], other_in[index], 1, 0)
        lay(outs[:pieces], 0, index, hidden.astype(BF16))
        grad = dot(own[:, cotangents], own_out[index], 1, 1)
        grad += dot(other[:, cotangents], other_out[index], 1, 1)
        lay(outs[:pieces], 1, index, grad.astype(BF16))


def gelu_kernel(n_depth, where, ins, outs, scratch):
    blocks = ins[0].shape[1]
    depth = where[1]
    for index in range(blocks):
        hidden, grad = ins[0][0, index].astype(F32), ins[0][1, index].astype(F32)
        for other in ins[1:]:
            hidden += other[0, index].astype(F32)
            grad += other[1, index].astype(F32)
        value, slope = gelu_parts(hidden)
        act, pre = value.astype(BF16), (grad * slope).astype(BF16)
        outs[0][0, index] = act
        outs[0][1, index] = pre
        for message in outs[1:]:
            message[index] = pre
    for k in range(1, len(outs)):
        owner = lax.rem(depth + k, n_depth) if k < n_depth else depth
        outs[k][blocks] = outs[0][0, owner]


def copy_kernel(where, ins, outs, scratch):
    outs[0][...] = ins[0][...]


def model_kernel(pieces, where, ins, outs, scratch):
    pairs, weights = ins[:pieces], ins[pieces:]
    pair = pairs[0]
    if pieces > 1:
        (pair,) = scratch
        rows = pairs[0].shape[2]
        for number, value in enumerate(pairs):
            pair[:, :, number * rows : (number + 1) * rows, :] = value[...]
    for rel, target in enumerate(outs):
        weight_in, weight_out = weights[2 * rel : 2 * rel + 2]
        out = grad = 0.0
        for index in range(pair.shape[1]):
            out += dot(pair[0, index], weight_out[index], 1, 0)
            grad += dot(pair[1, index], weight_in[index], 1, 1)
        target[0] = out.astype(BF16)
        target[1] = grad.astype(BF16)


def sum_kernel(where, ins, outs, scratch):
    for index in range(2):
        total = sum(value[index].astype(F32) for value in ins)
        if len(outs) == 1:
            outs[0][index] = total.astype(BF16)
        else:
            outs[index][...] = total.astype(BF16)


def early_kernel(near, where, ins, outs, scratch):
    all_tokens, all_cotangents, all_values = scratch
    own_in, own_out, other_in, other_out = outs
    blocks, part, width = own_in.shape
    features = own_out.shape[1]
    pairs, shares, came = ins[2 * near : 3 * near], ins[3 * near : 3 * near + 2], ins[3 * near + 2 :]
    rows = ins[0].shape[0]
    for rel in range(2):
        here = slice(rel * part, (rel + 1) * part)
        there = slice(rel * features, (rel + 1) * features)
        for number in range(near):
            at, source = slice(number * rows, (number + 1) * rows), ins[rel * near + number]
            all_tokens[at, here] = source[:, part_of(where, where[1], part)]
            all_cotangents[at, there] = source[:, features : 2 * features]
        for number in range(len(came)):
            at, source = slice(number * rows, (number + 1) * rows), shares[rel]
            start = (near + number) * rows
            all_tokens[start : start + rows, here] = source[at, :part]
            all_cotangents[start : start + rows, there] = source[at, part:]
    acts = [pair.at[0].at[where[1]] for pair in pairs] + [value.at[blocks] for value in came]
    pres = [[pair.at[1].at[index] for index in range(blocks)] for pair in pairs]
    pres += [[value.at[index] for index in range(blocks)] for value in came]

    def fill(sources):
        for number, source in enumerate(sources):
            all_values[number * rows : (number + 1) * rows, :] = source[...]

    for index in range(blocks):
        fill([value[index] for value in pres])
        term = dot(all_tokens[...], all_values[...], 0, 0)
        own_in[index] = term[:part]
        other_in[index] = term[part:].astype(BF16)
    fill(acts)
    term = dot(all_values[...], all_cotangents[...], 0, 0)
    own_out[...] = term[:, :features]
    other_out[...] = term[:, features:].astype(BF16)


def last_kernel(rel, groups, where, ins, outs, scratch):
    all_tokens, all_cotangents, all_values, held_in, held_out, semaphores = scratch
    own, *ins = ins
    shares, values, early = ins[: 2 * groups], ins[2 * groups : -2], ins[-2:]
    if rel:
        values, early = ins[2 * groups : -4], ins[-4:-2]
    rows, part = own.shape[0], all_tokens.shape[1]
    features, width = all_cotangents.shape[1], all_values.shape[1]
    blocks = held_in.shape[0]
    all_tokens[:rows, :] = own[:, part_of(where, where[1], part)]
    all_cotangents[:rows, :] = own[:, features : 2 * features]
    for number, share in enumerate(shares, 1):
        at = slice(number * rows, (number + 1) * rows)
        all_tokens[at, :] = share[:, :part]
        all_cotangents[at, :] = share[:, part:]
    copies = []

    def fill(index):
        row = 0
        for source in values:
            if len(source.shape) == 3:
                value = source[index]
            elif index < blocks:
                value = source[1, index]
            else:
                value = source[0, where[1]]
            all_values[row : row + value.shape[0], :] = value
            row += value.shape[0]

    def put(held, target, term):
        held[...] = term
        copies.append(pltpu.make_async_copy(held, target, semaphores.at[len(copies)]))
        copies[-1].start()

    core = where[0] if rel == 0 else 1 - where[0]
    for index in range(blocks):
        fill(index)
        before = early[0][index].astype(F32)
        term = dot(all_tokens[...], all_values[...], 0, 0) + before
        put(held_in.at[index], outs[0].at[:, block_of(where, rel, index, width)], term)
    fill(blocks)
    term = dot(all_values[...], all_cotangents[...], 0, 0) + early[1][...].astype(F32)
    at = pl.ds(pl.multiple_of(core * width, 128), width)
    put(held_out, outs[1].at[at, :], term)
    for copy in copies:
        copy.wait()


def shards(n_row, n_col, n_depth, tokens, weight_in, weight_out, output_grad):
    rows, features = tokens.shape
    part = features // n_depth
    blocks, width = n_depth, weight_in.shape[1] // (2 * n_depth)
    core = lax.axis_index("row") % 2
    depth = lax.axis_index("depth")
    chain = Chain(jnp.stack([core, depth]).astype(jnp.int32))

    def swap_cores(value):
        return lax.ppermute(value, "row", [(r, r ^ 1) for r in range(n_row)])

    def to_chip(value, k):
        return lax.ppermute(value, "row", [(r, (r + 2 * k) % n_row) for r in range(n_row)])

    def to_depth(value, k):
        return lax.ppermute(value, "depth", [(d, (d + k) % n_depth) for d in range(n_depth)])

    def to_col(value, k):
        return lax.ppermute(value, "col", [(c, (c + k) % n_col) for c in range(n_col)])

    single, pair_shape = shape(blocks, rows, width), shape(2, blocks, rows, width)
    model_shape = shape(2, rows, features)
    message_shape = shape(blocks + 1, rows, width)
    weight_shapes = [shape(blocks, features, width), shape(blocks, width, features)]
    groups = n_depth - 1
    last = n_col - 1
    own, other, shares = {}, {}, {}
    chip, crossed, pairs, came, model = {}, {}, {}, {}, {}

    def cross(stage):
        crossed[stage] = [
            [to_chip(value, k) for k in range(1, n_row // 2)] for value in chip[stage]
        ]

    ready = {}
    share_shapes = [shape(rows, part + features)] * groups
    semaphores = [pltpu.SemaphoreType.DMA((2 * blocks,))]

    def send_shares(stage, values):
        shares[stage] = [to_depth(value, k) for k, value in enumerate(values, 1)]
        ready["T", stage] = shares[stage]

    kept_weights = chain(
        fetch_kernel,
        [weight_in, weight_out],
        weight_shapes,
        scratch=semaphores,
        specs=[IN_HBM] * 2,
        limit=49,
    )
    other_weights = [swap_cores(value) for value in kept_weights]
    hidden, grad, own[0], *results = chain(
        other_kernel,
        [tokens, output_grad] + kept_weights,
        [single, single, shape(rows, 2 * features)] + share_shapes,
    )
    send_shares(0, results)
    swapped = [swap_cores(value) for value in (hidden, grad)]
    *own_weights, hidden, grad = chain(
        own_kernel,
        [own[0], weight_in, weight_out],
        weight_shapes + [single, single],
        scratch=semaphores,
        specs=[IN_VMEM] + [IN_HBM] * 2,
        limit=46,
    )
    chip[0] = chain(join_kernel, [hidden, grad] + swapped, [pair_shape])
    cross(0)
    other[0] = swap_cores(own[0])
    ready["O", 0] = [other[0]]
    own[1] = to_col(own[0], 1)
    raw, early_shares = {1: own[1]}, []

    def arrive_step(stage, after):
        raw[stage] = to_col(raw[stage - 1], 1)
        near, stacked = [raw[stage]], []
        if stage == last - 1:
            near += [value for earlier in range(stage) for value in shares[earlier]]
            stacked = [shape(stage * groups * rows, part + features)]
        own[stage], *results = chain(
            arrive_kernel, near, [shape(rows, 2 * features)] + stacked, after=after
        )
        if results:
            early_shares.extend(results + [swap_cores(results[0])])

    def hidden_step(stage, after):
        other[stage] = swap_cores(own[stage])
        sends = stage <= last - HOPS
        pieces = HALVES if stage == last else 1
        results = chain(
            functools.partial(hidden_kernel, stage == 1, pieces),
            [own[stage], other[stage]] + own_weights + other_weights,
            [shape(2, blocks, rows // pieces, width)] * pieces
            + (share_shapes if sends else [])
            + (weight_shapes if stage == 1 else []),
            after=after,
        )
        chip[stage], results = results[:pieces], results[pieces:]
        if sends:
            send_shares(stage, results[:groups])
        else:
            shares[stage] = [to_col(value, 1) for value in shares[stage - 1]]
            ready["T", stage] = shares[stage]
        if stage == 1:
            other_weights[:] = results[groups * sends :]
        cross(stage)

    def gelu_step(step, after):
        stage = min(step, last)
        piece = step - stage
        size = chip[stage][piece].shape[2]
        inputs = [chip[stage][piece]] + crossed[stage][piece]
        outputs = [shape(2, blocks, size, width)] + [shape(blocks + 1, size, width)] * groups
        if stage == last:
            outputs += [shape(blocks + 1, size, width)]
        pair, *messages = chain(
            functools.partial(gelu_kernel, n_depth), inputs, outputs, after=after
        )
        pairs.setdefault(stage, []).append(pair)
        arrived = [to_depth(value, k) for k, value in enumerate(messages[:groups], 1)]
        came.setdefault(stage, []).append(arrived)
        ready["Y", step] = arrived
        if stage == last:
            late.append(swap_cores(messages[groups]))

    def pass_step(stage, after):
        for value in came[last - 1][0]:
            (copied,) = chain(copy_kernel, [value], [message_shape], after=after)
            late_far.append(swap_cores(copied))
        ready["C", 0] = late_far[:]

    def model_step(stage, after):
        pieces = len(pairs[stage])
        mine, theirs = chain(
            functools.partial(model_kernel, pieces),
            pairs[stage] + own_weights + other_weights,
            [model_shape] * 2,
            after=after,
            scratch=[pltpu.VMEM(pair_shape.shape, BF16)] if pieces > 1 else [],
        )
        model[stage] = [mine, swap_cores(theirs)]
        ready["M", stage] = model[stage][1:]

    def sum_step(stage, after):
        brought = ring.get(stage - 1, []) if RING else []
        (total,) = chain(sum_kernel, model[stage] + brought, [model_shape], after=after)
        if RING:
            ring[stage] = [to_col(total, 1)]
        else:
            ring[stage] = [to_col(total, n_col - stage)]
        ready["S", stage] = ring[stage]

    def early_step(stage, after):
        count = rows * (last + (last - 1) * groups)
        term_sizes = [(blocks, part, width), (width, features)]
        near = list(range(last))
        values = [source[number] for source in (own, other) for number in near]
        values += [pairs[number][0] for number in near] + early_shares
        values += [value for number in range(last - 1) for value in came[number][0]]
        first_in, first_out, sent_in, sent_out = chain(
            functools.partial(early_kernel, last),
            values,
            [shape(*size, kind=kind) for kind in (F32, BF16) for size in term_sizes],
            after=after,
            scratch=[
                pltpu.VMEM((count, 2 * part), BF16),
                pltpu.VMEM((count, 2 * features), BF16),
                pltpu.VMEM((count, width), BF16),
            ],
            limit=24,
        )
        early.extend([first_in, first_out, swap_cores(sent_in), swap_cores(sent_out)])
        ready["E", 0] = early[2:]

    def last_step(rel, after):
        chunk = [own[last]] + shares[last - 1] + shares[last]
        arrived = [half[k] for k in range(groups) for half in came[last]]
        if rel == 0:
            values = pairs[last] + came[last - 1][0] + arrived
            swapped.extend(swap_cores(value) for value in arrived)
        else:
            values = late + late_far + swapped
        inputs = chunk + values + early[2 * rel : 2 * rel + 2] + results[2:]
        count = rows * (1 + 2 * groups)
        grads = [shape(part, 2 * blocks * width, kind=F32), shape(2 * width, features, kind=F32)]
        results[2:] = chain(
            functools.partial(last_kernel, rel, groups),
            inputs,
            grads,
            after=after,
            scratch=[
                pltpu.VMEM((count, part), BF16),
                pltpu.VMEM((count, features), BF16),
                pltpu.VMEM((count, width), BF16),
                pltpu.VMEM((blocks, part, width), F32),
                pltpu.VMEM((width, features), F32),
                pltpu.SemaphoreType.DMA((blocks + 1,)),
            ],
            specs=[IN_VMEM] * (len(inputs) - 2 * rel) + [IN_HBM] * (2 * rel),
            limit=20,
            to=IN_HBM,
            filled=2 * rel,
        )

    def final_step(stage, after):
        values = model[0] + (ring[last] if RING else [v for s in range(1, n_col) for v in ring[s]])
        results[:2] = chain(sum_kernel, values, [shape(rows, features)] * 2, after=after)

    ring, early, results = {}, [], [None, None]
    late, late_far, swapped = [], [], []
    steps = {
        "U": arrive_step,
        "H": hidden_step,
        "G": gelu_step,
        "C": pass_step,
        "M": model_step,
        "S": sum_step,
        "E": early_step,
        "L": last_step,
        "F": final_step,
    }
    order, waits = PLANS.get(last) or default_plan(last)
    for name, stage in order:
        chain.flops = COSTS.get((name, stage), 1000)
        steps[name](stage, [v for key in waits.get((name, stage), ()) for v in ready[key]])
    return tuple(results)


def plain_shards(tokens, weight_in, weight_out, output_grad):
    x_panel = lax.all_gather(tokens, "col", axis=0, tiled=True)
    dy_panel = lax.all_gather(output_grad, "col", axis=0, tiled=True)

    def hidden_total(term):
        return lax.psum(term.astype(BF16), "row").astype(F32)

    def scattered(term, axis):
        return lax.psum_scatter(term.astype(BF16), axis, scatter_dimension=0, tiled=True)

    value, slope = gelu_parts(hidden_total(dot(x_panel, weight_in, 1, 0)))
    act = value.astype(BF16)
    pre = (hidden_total(dot(dy_panel, weight_out, 1, 1)) * slope).astype(BF16)
    return (
        scattered(dot(act, weight_out, 1, 0), "col"),
        scattered(dot(pre, weight_in, 1, 1), "col"),
        scattered(dot(x_panel, pre, 0, 0), "depth").astype(F32),
        scattered(dot(act, dy_panel, 0, 0), "depth").astype(F32),
    )


def solution(mesh):
    placed = (
        P(("col", "depth"), "row"),
        P("row", "col"),
        P("col", "row"),
        P(("col", "depth"), "row"),
    )
    sizes = (mesh.shape["row"], mesh.shape["col"], mesh.shape["depth"])

    def local(tokens, weight_in, weight_out, output_grad):
        arrays = (tokens, weight_in, weight_out, output_grad)
        n_row, n_col, n_depth = sizes
        width, part = weight_in.shape[1] // (2 * n_depth), tokens.shape[1] // n_depth
        fits = width % 128 == 0 and part % 128 == 0 and tokens.shape[0] % (16 * HALVES) == 0
        if fits and n_row % 2 == 0 and n_col > 2 and n_depth > 1:
            return shards(*sizes, *arrays)
        return plain_shards(*arrays)

    return jax.shard_map(
        local,
        mesh=mesh,
        in_specs=placed,
        out_specs=(
            P(("col", "depth"), "row"),
            P(("col", "depth"), "row"),
            P(("row", "depth"), "col"),
            P(("col", "depth"), "row"),
        ),
        check_vma=False,
    )
```

```python
import functools

import jax
import jax.numpy as jnp
from jax import lax
from jax.experimental import pallas as pl
from jax.experimental.pallas import tpu as pltpu
from jax.sharding import PartitionSpec as P

BF16, F32 = jnp.bfloat16, jnp.float32
MIB = 1024 * 1024
IN_VMEM = pl.BlockSpec(memory_space=pltpu.VMEM)
IN_SMEM = pl.BlockSpec(memory_space=pltpu.SMEM)
IN_HBM = pl.BlockSpec(memory_space=pltpu.HBM)
ANYWHERE = pl.BlockSpec(memory_space=pl.ANY)
TOKEN = jax.ShapeDtypeStruct((8, 128), F32)


RING = True
HOPS = 0
HALVES = 2
COSTS = {('G', 4): 3000000000}
PLANS = {
    3: (
        (
            ("H", 1), ("G", 0), ("U", 2), ("M", 0), ("H", 2), ("G", 1),
            ("U", 3), ("M", 1), ("H", 3), ("G", 2), ("S", 1), ("M", 2),
            ("E", 0), ("G", 3), ("G", 4), ("C", 0), ("M", 3), ("S", 2),
            ("S", 3), ("L", 0), ("L", 1), ("F", 0),
        ),
        {
            ("G", 0): (("O", 0),),
            ("U", 2): (("T", 1),),
            ("U", 3): (("T", 2),),
            ("G", 1): (("Y", 0), ("M", 0),),
            ("G", 2): (("Y", 1),),
            ("G", 3): (("T", 3),),
        },
    ),
}


def default_plan(last):
    order = [("H", 1), ("G", 0)]
    for stage in range(2, last + 1):
        order += [("U", stage), ("M", stage - 2), ("H", stage), ("G", stage - 1)]
        order += [("S", stage - 2)] if stage > 2 else []
    order += [("M", last - 1), ("E", 0), ("C", 0)]
    order += [("G", last + half) for half in range(HALVES)]
    order += [("M", last), ("S", last - 1), ("S", last)]
    return order + [("L", 0), ("L", 1), ("F", 0)], {}


def gelu_parts(hidden_pre):
    normal_cdf = 0.5 * (1.0 + lax.erf(hidden_pre * 0.7071067811865476))
    normal_pdf = jnp.exp(-0.5 * hidden_pre * hidden_pre) * 0.3989422804014327
    return (hidden_pre * normal_cdf, normal_cdf + hidden_pre * normal_pdf)


def dot(left, right, left_dim, right_dim):
    return lax.dot_general(
        left, right, (((left_dim,), (right_dim,)), ((), ())), preferred_element_type=F32
    )


def shape(*sizes, kind=BF16):
    return jax.ShapeDtypeStruct(sizes, kind)


class Chain:
    def __init__(self, where):
        self.where = where
        self.token = jnp.zeros(TOKEN.shape, TOKEN.dtype)
        self.flops = 1000

    def __call__(
        self,
        kernel,
        inputs,
        out_shapes,
        after=(),
        scratch=(),
        limit=16,
        specs=None,
        to=IN_VMEM,
        filled=0,
    ):
        n_in, n_after, n_out = len(inputs), len(after) + 1, len(out_shapes)

        def body(where, *refs):
            ins = refs[:n_in]
            outs = refs[n_in + n_after : n_in + n_after + n_out]
            token = refs[n_in + n_after + n_out]
            kernel(where, ins, outs, refs[n_in + n_after + n_out + 1 :])
            token[...] = jnp.zeros(token.shape, token.dtype)

        *results, self.token = pl.pallas_call(
            body,
            in_specs=[IN_SMEM] + (specs or [IN_VMEM] * n_in) + [ANYWHERE] * n_after,
            out_specs=[to] * n_out + [IN_VMEM],
            out_shape=list(out_shapes) + [TOKEN],
            scratch_shapes=list(scratch),
            input_output_aliases={1 + n_in - filled + k: k for k in range(filled)},
            compiler_params=pltpu.CompilerParams(vmem_limit_bytes=limit * MIB),
            cost_estimate=pl.CostEstimate(
                flops=self.flops, bytes_accessed=1000, transcendentals=0
            ),
        )(self.where, *inputs, *after, self.token)
        return results


def block_of(where, rel, index, width):
    core = where[0] if rel == 0 else 1 - where[0]
    return pl.ds(pl.multiple_of((2 * index + core) * width, 128), width)


def part_of(where, owner, part):
    return pl.ds(pl.multiple_of(owner * part, 128), part)


def cut_shares(where, both, features, messages):
    for k, message in enumerate(messages, 1):
        part = message.shape[1] - features
        owner = lax.rem(where[1] + k, len(messages) + 1)
        message[:, :part] = both[:, part_of(where, owner, part)]
        message[:, part:] = both[:, features : 2 * features]


def fetch(where, rel, sources, targets, semaphores):
    from_in, from_out = sources
    weight_in, weight_out = targets
    copies = []
    for index in range(weight_in.shape[0]):
        cut = block_of(where, rel, index, weight_in.shape[2])
        for source, target in (
            (from_in.at[:, cut], weight_in.at[index]),
            (from_out.at[cut, :], weight_out.at[index]),
        ):
            copies.append(pltpu.make_async_copy(source, target, semaphores.at[len(copies)]))
            copies[-1].start()
    return copies


def fetch_kernel(where, ins, outs, scratch):
    for copy in fetch(where, 1, ins, outs, scratch[0]):
        copy.wait()


def other_kernel(where, ins, outs, scratch):
    *chunk, weight_in, weight_out = ins
    hidden, grad, both, *messages = outs
    features = weight_in.shape[1]
    both[:, :features] = chunk[0][...]
    both[:, features:] = chunk[1][...]
    cut_shares(where, both, features, messages)
    for index in range(weight_in.shape[0]):
        hidden[index] = dot(chunk[0][...], weight_in[index], 1, 0).astype(BF16)
        grad[index] = dot(chunk[1][...], weight_out[index], 1, 1).astype(BF16)


def own_kernel(where, ins, outs, scratch):
    both, *sources = ins
    copies = fetch(where, 0, sources, outs[:2], scratch[0])
    features = outs[0].shape[1]
    for index in range(outs[0].shape[0]):
        for which in range(2):
            copies[2 * index + which].wait()
            left = both[:, which * features : (which + 1) * features]
            outs[2 + which][index] = dot(left, outs[which][index], 1, which).astype(BF16)


def join_kernel(where, ins, outs, scratch):
    for which in range(2):
        total = ins[which][...].astype(F32) + ins[2 + which][...].astype(F32)
        outs[0][which] = total.astype(BF16)


def arrive_kernel(where, ins, outs, scratch):
    outs[0][...] = ins[0][...]
    for number, value in enumerate(ins[1:]):
        rows = value.shape[0]
        outs[1][number * rows : (number + 1) * rows, :] = value[...]


def lay(targets, which, index, value):
    rows = targets[0].shape[2]
    for number, target in enumerate(targets):
        target[which, index] = value[number * rows : (number + 1) * rows]


def hidden_kernel(keep, pieces, where, ins, outs, scratch):
    own, other, own_in, own_out, other_in, other_out = ins
    if keep:
        outs[-2][...] = other_in[...]
        outs[-1][...] = other_out[...]
    cut_shares(where, own, own_in.shape[1], outs[pieces : len(outs) - 2 * keep])
    features = own_in.shape[1]
    tokens, cotangents = slice(0, features), slice(features, 2 * features)
    for index in range(own_in.shape[0]):
        hidden = dot(own[:, tokens], own_in[index], 1, 0)
        hidden += dot(other[:, tokens], other_in[index], 1, 0)
        lay(outs[:pieces], 0, index, hidden.astype(BF16))
        grad = dot(own[:, cotangents], own_out[index], 1, 1)
        grad += dot(other[:, cotangents], other_out[index], 1, 1)
        lay(outs[:pieces], 1, index, grad.astype(BF16))


def gelu_kernel(n_depth, where, ins, outs, scratch):
    blocks = ins[0].shape[1]
    depth = where[1]
    for index in range(blocks):
        hidden, grad = ins[0][0, index].astype(F32), ins[0][1, index].astype(F32)
        for other in ins[1:]:
            hidden += other[0, index].astype(F32)
            grad += other[1, index].astype(F32)
        value, slope = gelu_parts(hidden)
        act, pre = value.astype(BF16), (grad * slope).astype(BF16)
        outs[0][0, index] = act
        outs[0][1, index] = pre
        for message in outs[1:]:
            message[index] = pre
    for k in range(1, len(outs)):
        owner = lax.rem(depth + k, n_depth) if k < n_depth else depth
        outs[k][blocks] = outs[0][0, owner]


def copy_kernel(where, ins, outs, scratch):
    outs[0][...] = ins[0][...]


def model_kernel(pieces, where, ins, outs, scratch):
    pairs, weights = ins[:pieces], ins[pieces:]
    pair = pairs[0]
    if pieces > 1:
        (pair,) = scratch
        rows = pairs[0].shape[2]
        for number, value in enumerate(pairs):
            pair[:, :, number * rows : (number + 1) * rows, :] = value[...]
    for rel, target in enumerate(outs):
        weight_in, weight_out = weights[2 * rel : 2 * rel + 2]
        out = grad = 0.0
        for index in range(pair.shape[1]):
            out += dot(pair[0, index], weight_out[index], 1, 0)
            grad += dot(pair[1, index], weight_in[index], 1, 1)
        target[0] = out.astype(BF16)
        target[1] = grad.astype(BF16)


def sum_kernel(where, ins, outs, scratch):
    for index in range(2):
        total = sum(value[index].astype(F32) for value in ins)
        if len(outs) == 1:
            outs[0][index] = total.astype(BF16)
        else:
            outs[index][...] = total.astype(BF16)


def early_kernel(near, where, ins, outs, scratch):
    all_tokens, all_cotangents, all_values = scratch
    own_in, own_out, other_in, other_out = outs
    blocks, part, width = own_in.shape
    features = own_out.shape[1]
    pairs, shares, came = ins[2 * near : 3 * near], ins[3 * near : 3 * near + 2], ins[3 * near + 2 :]
    rows = ins[0].shape[0]
    for rel in range(2):
        here = slice(rel * part, (rel + 1) * part)
        there = slice(rel * features, (rel + 1) * features)
        for number in range(near):
            at, source = slice(number * rows, (number + 1) * rows), ins[rel * near + number]
            all_tokens[at, here] = source[:, part_of(where, where[1], part)]
            all_cotangents[at, there] = source[:, features : 2 * features]
        for number in range(len(came)):
            at, source = slice(number * rows, (number + 1) * rows), shares[rel]
            start = (near + number) * rows
            all_tokens[start : start + rows, here] = source[at, :part]
            all_cotangents[start : start + rows, there] = source[at, part:]
    acts = [pair.at[0].at[where[1]] for pair in pairs] + [value.at[blocks] for value in came]
    pres = [[pair.at[1].at[index] for index in range(blocks)] for pair in pairs]
    pres += [[value.at[index] for index in range(blocks)] for value in came]

    def fill(sources):
        for number, source in enumerate(sources):
            all_values[number * rows : (number + 1) * rows, :] = source[...]

    for index in range(blocks):
        fill([value[index] for value in pres])
        term = dot(all_tokens[...], all_values[...], 0, 0)
        own_in[index] = term[:part]
        other_in[index] = term[part:].astype(BF16)
    fill(acts)
    term = dot(all_values[...], all_cotangents[...], 0, 0)
    own_out[...] = term[:, :features]
    other_out[...] = term[:, features:].astype(BF16)


def last_kernel(rel, groups, where, ins, outs, scratch):
    all_tokens, all_cotangents, all_values, held_in, held_out, semaphores = scratch
    own, *ins = ins
    shares, values, early = ins[: 2 * groups], ins[2 * groups : -2], ins[-2:]
    if rel:
        values, early = ins[2 * groups : -4], ins[-4:-2]
    rows, part = own.shape[0], all_tokens.shape[1]
    features, width = all_cotangents.shape[1], all_values.shape[1]
    blocks = held_in.shape[0]
    all_tokens[:rows, :] = own[:, part_of(where, where[1], part)]
    all_cotangents[:rows, :] = own[:, features : 2 * features]
    for number, share in enumerate(shares, 1):
        at = slice(number * rows, (number + 1) * rows)
        all_tokens[at, :] = share[:, :part]
        all_cotangents[at, :] = share[:, part:]
    copies = []

    def fill(index):
        row = 0
        for source in values:
            if len(source.shape) == 3:
                value = source[index]
            elif index < blocks:
                value = source[1, index]
            else:
                value = source[0, where[1]]
            all_values[row : row + value.shape[0], :] = value
            row += value.shape[0]

    def put(held, target, term):
        held[...] = term
        copies.append(pltpu.make_async_copy(held, target, semaphores.at[len(copies)]))
        copies[-1].start()

    core = where[0] if rel == 0 else 1 - where[0]
    for index in range(blocks):
        fill(index)
        before = early[0][index].astype(F32)
        term = dot(all_tokens[...], all_values[...], 0, 0) + before
        put(held_in.at[index], outs[0].at[:, block_of(where, rel, index, width)], term)
    fill(blocks)
    term = dot(all_values[...], all_cotangents[...], 0, 0) + early[1][...].astype(F32)
    at = pl.ds(pl.multiple_of(core * width, 128), width)
    put(held_out, outs[1].at[at, :], term)
    for copy in copies:
        copy.wait()


def shards(n_row, n_col, n_depth, tokens, weight_in, weight_out, output_grad):
    rows, features = tokens.shape
    part = features // n_depth
    blocks, width = n_depth, weight_in.shape[1] // (2 * n_depth)
    core = lax.axis_index("row") % 2
    depth = lax.axis_index("depth")
    chain = Chain(jnp.stack([core, depth]).astype(jnp.int32))

    def swap_cores(value):
        return lax.ppermute(value, "row", [(r, r ^ 1) for r in range(n_row)])

    def to_chip(value, k):
        return lax.ppermute(value, "row", [(r, (r + 2 * k) % n_row) for r in range(n_row)])

    def to_depth(value, k):
        return lax.ppermute(value, "depth", [(d, (d + k) % n_depth) for d in range(n_depth)])

    def to_col(value, k):
        return lax.ppermute(value, "col", [(c, (c + k) % n_col) for c in range(n_col)])

    single, pair_shape = shape(blocks, rows, width), shape(2, blocks, rows, width)
    model_shape = shape(2, rows, features)
    message_shape = shape(blocks + 1, rows, width)
    weight_shapes = [shape(blocks, features, width), shape(blocks, width, features)]
    groups = n_depth - 1
    last = n_col - 1
    own, other, shares = {}, {}, {}
    chip, crossed, pairs, came, model = {}, {}, {}, {}, {}

    def cross(stage):
        crossed[stage] = [
            [to_chip(value, k) for k in range(1, n_row // 2)] for value in chip[stage]
        ]

    ready = {}
    share_shapes = [shape(rows, part + features)] * groups
    semaphores = [pltpu.SemaphoreType.DMA((2 * blocks,))]

    def send_shares(stage, values):
        shares[stage] = [to_depth(value, k) for k, value in enumerate(values, 1)]
        ready["T", stage] = shares[stage]

    kept_weights = chain(
        fetch_kernel,
        [weight_in, weight_out],
        weight_shapes,
        scratch=semaphores,
        specs=[IN_HBM] * 2,
        limit=49,
    )
    other_weights = [swap_cores(value) for value in kept_weights]
    hidden, grad, own[0], *results = chain(
        other_kernel,
        [tokens, output_grad] + kept_weights,
        [single, single, shape(rows, 2 * features)] + share_shapes,
    )
    send_shares(0, results)
    swapped = [swap_cores(value) for value in (hidden, grad)]
    *own_weights, hidden, grad = chain(
        own_kernel,
        [own[0], weight_in, weight_out],
        weight_shapes + [single, single],
        scratch=semaphores,
        specs=[IN_VMEM] + [IN_HBM] * 2,
        limit=46,
    )
    chip[0] = chain(join_kernel, [hidden, grad] + swapped, [pair_shape])
    cross(0)
    other[0] = swap_cores(own[0])
    ready["O", 0] = [other[0]]
    own[1] = to_col(own[0], 1)
    raw, early_shares = {1: own[1]}, []

    def arrive_step(stage, after):
        raw[stage] = to_col(raw[stage - 1], 1)
        near, stacked = [raw[stage]], []
        if stage == last - 1:
            near += [value for earlier in range(stage) for value in shares[earlier]]
            stacked = [shape(stage * groups * rows, part + features)]
        own[stage], *results = chain(
            arrive_kernel, near, [shape(rows, 2 * features)] + stacked, after=after
        )
        if results:
            early_shares.extend(results + [swap_cores(results[0])])

    def hidden_step(stage, after):
        other[stage] = swap_cores(own[stage])
        sends = stage <= last - HOPS
        pieces = HALVES if stage == last else 1
        results = chain(
            functools.partial(hidden_kernel, stage == 1, pieces),
            [own[stage], other[stage]] + own_weights + other_weights,
            [shape(2, blocks, rows // pieces, width)] * pieces
            + (share_shapes if sends else [])
            + (weight_shapes if stage == 1 else []),
            after=after,
        )
        chip[stage], results = results[:pieces], results[pieces:]
        if sends:
            send_shares(stage, results[:groups])
        else:
            shares[stage] = [to_col(value, 1) for value in shares[stage - 1]]
            ready["T", stage] = shares[stage]
        if stage == 1:
            other_weights[:] = results[groups * sends :]
        cross(stage)

    def gelu_step(step, after):
        stage = min(step, last)
        piece = step - stage
        size = chip[stage][piece].shape[2]
        inputs = [chip[stage][piece]] + crossed[stage][piece]
        outputs = [shape(2, blocks, size, width)] + [shape(blocks + 1, size, width)] * groups
        if stage == last:
            outputs += [shape(blocks + 1, size, width)]
        pair, *messages = chain(
            functools.partial(gelu_kernel, n_depth), inputs, outputs, after=after
        )
        pairs.setdefault(stage, []).append(pair)
        arrived = [to_depth(value, k) for k, value in enumerate(messages[:groups], 1)]
        came.setdefault(stage, []).append(arrived)
        ready["Y", step] = arrived
        if stage == last:
            late.append(swap_cores(messages[groups]))

    def pass_step(stage, after):
        for value in came[last - 1][0]:
            (copied,) = chain(copy_kernel, [value], [message_shape], after=after)
            late_far.append(swap_cores(copied))
        ready["C", 0] = late_far[:]

    def model_step(stage, after):
        pieces = len(pairs[stage])
        mine, theirs = chain(
            functools.partial(model_kernel, pieces),
            pairs[stage] + own_weights + other_weights,
            [model_shape] * 2,
            after=after,
            scratch=[pltpu.VMEM(pair_shape.shape, BF16)] if pieces > 1 else [],
        )
        model[stage] = [mine, swap_cores(theirs)]
        ready["M", stage] = model[stage][1:]

    def sum_step(stage, after):
        brought = ring.get(stage - 1, []) if RING else []
        (total,) = chain(sum_kernel, model[stage] + brought, [model_shape], after=after)
        if RING:
            ring[stage] = [to_col(total, 1)]
        else:
            ring[stage] = [to_col(total, n_col - stage)]
        ready["S", stage] = ring[stage]

    def early_step(stage, after):
        count = rows * (last + (last - 1) * groups)
        term_sizes = [(blocks, part, width), (width, features)]
        near = list(range(last))
        values = [source[number] for source in (own, other) for number in near]
        values += [pairs[number][0] for number in near] + early_shares
        values += [value for number in range(last - 1) for value in came[number][0]]
        first_in, first_out, sent_in, sent_out = chain(
            functools.partial(early_kernel, last),
            values,
            [shape(*size, kind=kind) for kind in (F32, BF16) for size in term_sizes],
            after=after,
            scratch=[
                pltpu.VMEM((count, 2 * part), BF16),
                pltpu.VMEM((count, 2 * features), BF16),
                pltpu.VMEM((count, width), BF16),
            ],
            limit=24,
        )
        early.extend([first_in, first_out, swap_cores(sent_in), swap_cores(sent_out)])
        ready["E", 0] = early[2:]

    def last_step(rel, after):
        chunk = [own[last]] + shares[last - 1] + shares[last]
        arrived = [half[k] for k in range(groups) for half in came[last]]
        if rel == 0:
            values = pairs[last] + came[last - 1][0] + arrived
            swapped.extend(swap_cores(value) for value in arrived)
        else:
            values = late + late_far + swapped
        inputs = chunk + values + early[2 * rel : 2 * rel + 2] + results[2:]
        count = rows * (1 + 2 * groups)
        grads = [shape(part, 2 * blocks * width, kind=F32), shape(2 * width, features, kind=F32)]
        results[2:] = chain(
            functools.partial(last_kernel, rel, groups),
            inputs,
            grads,
            after=after,
            scratch=[
                pltpu.VMEM((count, part), BF16),
                pltpu.VMEM((count, features), BF16),
                pltpu.VMEM((count, width), BF16),
                pltpu.VMEM((blocks, part, width), F32),
                pltpu.VMEM((width, features), F32),
                pltpu.SemaphoreType.DMA((blocks + 1,)),
            ],
            specs=[IN_VMEM] * (len(inputs) - 2 * rel) + [IN_HBM] * (2 * rel),
            limit=20,
            to=IN_HBM,
            filled=2 * rel,
        )

    def final_step(stage, after):
        values = model[0] + (ring[last] if RING else [v for s in range(1, n_col) for v in ring[s]])
        results[:2] = chain(sum_kernel, values, [shape(rows, features)] * 2, after=after)

    ring, early, results = {}, [], [None, None]
    late, late_far, swapped = [], [], []
    steps = {
        "U": arrive_step,
        "H": hidden_step,
        "G": gelu_step,
        "C": pass_step,
        "M": model_step,
        "S": sum_step,
        "E": early_step,
        "L": last_step,
        "F": final_step,
    }
    order, waits = PLANS.get(last) or default_plan(last)
    for name, stage in order:
        chain.flops = COSTS.get((name, stage), 1000)
        steps[name](stage, [v for key in waits.get((name, stage), ()) for v in ready[key]])
    return tuple(results)


def plain_shards(tokens, weight_in, weight_out, output_grad):
    x_panel = lax.all_gather(tokens, "col", axis=0, tiled=True)
    dy_panel = lax.all_gather(output_grad, "col", axis=0, tiled=True)

    def hidden_total(term):
        return lax.psum(term.astype(BF16), "row").astype(F32)

    def scattered(term, axis):
        return lax.psum_scatter(term.astype(BF16), axis, scatter_dimension=0, tiled=True)

    value, slope = gelu_parts(hidden_total(dot(x_panel, weight_in, 1, 0)))
    act = value.astype(BF16)
    pre = (hidden_total(dot(dy_panel, weight_out, 1, 1)) * slope).astype(BF16)
    return (
        scattered(dot(act, weight_out, 1, 0), "col"),
        scattered(dot(pre, weight_in, 1, 1), "col"),
        scattered(dot(x_panel, pre, 0, 0), "depth").astype(F32),
        scattered(dot(act, dy_panel, 0, 0), "depth").astype(F32),
    )


def solution(mesh):
    placed = (
        P(("col", "depth"), "row"),
        P("row", "col"),
        P("col", "row"),
        P(("col", "depth"), "row"),
    )
    sizes = (mesh.shape["row"], mesh.shape["col"], mesh.shape["depth"])

    def local(tokens, weight_in, weight_out, output_grad):
        arrays = (tokens, weight_in, weight_out, output_grad)
        n_row, n_col, n_depth = sizes
        width, part = weight_in.shape[1] // (2 * n_depth), tokens.shape[1] // n_depth
        fits = width % 128 == 0 and part % 128 == 0 and tokens.shape[0] % (16 * HALVES) == 0
        if fits and n_row % 2 == 0 and n_col > 2 and n_depth > 1:
            return shards(*sizes, *arrays)
        return plain_shards(*arrays)

    return jax.shard_map(
        local,
        mesh=mesh,
        in_specs=placed,
        out_specs=(
            P(("col", "depth"), "row"),
            P(("col", "depth"), "row"),
            P(("row", "depth"), "col"),
            P(("col", "depth"), "row"),
        ),
        check_vma=False,
    )
```

```python
import functools

import jax
import jax.numpy as jnp
from jax import lax
from jax.experimental import pallas as pl
from jax.experimental.pallas import tpu as pltpu
from jax.sharding import PartitionSpec as P

BF16, F32 = jnp.bfloat16, jnp.float32
MIB = 1024 * 1024
IN_VMEM = pl.BlockSpec(memory_space=pltpu.VMEM)
IN_SMEM = pl.BlockSpec(memory_space=pltpu.SMEM)
IN_HBM = pl.BlockSpec(memory_space=pltpu.HBM)
ANYWHERE = pl.BlockSpec(memory_space=pl.ANY)
TOKEN = jax.ShapeDtypeStruct((8, 128), F32)


RING = True
HOPS = 0
HALVES = 2
COSTS = {('G', 4): 3000000000}
PLANS = {
    3: (
        (
            ("H", 1), ("G", 0), ("U", 2), ("M", 0), ("H", 2), ("G", 1),
            ("U", 3), ("M", 1), ("H", 3), ("G", 2), ("S", 1), ("M", 2),
            ("E", 0), ("G", 3), ("G", 4), ("C", 0), ("M", 3), ("S", 2),
            ("S", 3), ("L", 0), ("L", 1), ("F", 0),
        ),
        {
            ("G", 0): (("O", 0),),
            ("U", 2): (("T", 1),),
            ("U", 3): (("T", 2),),
            ("G", 1): (("Y", 0), ("M", 0),),
            ("G", 2): (("Y", 1),),
            ("G", 3): (("T", 3),),
            ("C", 0): (("S", 1),),
        },
    ),
}


def default_plan(last):
    order = [("H", 1), ("G", 0)]
    for stage in range(2, last + 1):
        order += [("U", stage), ("M", stage - 2), ("H", stage), ("G", stage - 1)]
        order += [("S", stage - 2)] if stage > 2 else []
    order += [("M", last - 1), ("E", 0), ("C", 0)]
    order += [("G", last + half) for half in range(HALVES)]
    order += [("M", last), ("S", last - 1), ("S", last)]
    return order + [("L", 0), ("L", 1), ("F", 0)], {}


def gelu_parts(hidden_pre):
    normal_cdf = 0.5 * (1.0 + lax.erf(hidden_pre * 0.7071067811865476))
    normal_pdf = jnp.exp(-0.5 * hidden_pre * hidden_pre) * 0.3989422804014327
    return (hidden_pre * normal_cdf, normal_cdf + hidden_pre * normal_pdf)


def dot(left, right, left_dim, right_dim):
    return lax.dot_general(
        left, right, (((left_dim,), (right_dim,)), ((), ())), preferred_element_type=F32
    )


def shape(*sizes, kind=BF16):
    return jax.ShapeDtypeStruct(sizes, kind)


class Chain:
    def __init__(self, where):
        self.where = where
        self.token = jnp.zeros(TOKEN.shape, TOKEN.dtype)
        self.flops = 1000

    def __call__(
        self,
        kernel,
        inputs,
        out_shapes,
        after=(),
        scratch=(),
        limit=16,
        specs=None,
        to=IN_VMEM,
        filled=0,
    ):
        n_in, n_after, n_out = len(inputs), len(after) + 1, len(out_shapes)

        def body(where, *refs):
            ins = refs[:n_in]
            outs = refs[n_in + n_after : n_in + n_after + n_out]
            token = refs[n_in + n_after + n_out]
            kernel(where, ins, outs, refs[n_in + n_after + n_out + 1 :])
            token[...] = jnp.zeros(token.shape, token.dtype)

        *results, self.token = pl.pallas_call(
            body,
            in_specs=[IN_SMEM] + (specs or [IN_VMEM] * n_in) + [ANYWHERE] * n_after,
            out_specs=[to] * n_out + [IN_VMEM],
            out_shape=list(out_shapes) + [TOKEN],
            scratch_shapes=list(scratch),
            input_output_aliases={1 + n_in - filled + k: k for k in range(filled)},
            compiler_params=pltpu.CompilerParams(vmem_limit_bytes=limit * MIB),
            cost_estimate=pl.CostEstimate(
                flops=self.flops, bytes_accessed=1000, transcendentals=0
            ),
        )(self.where, *inputs, *after, self.token)
        return results


def block_of(where, rel, index, width):
    core = where[0] if rel == 0 else 1 - where[0]
    return pl.ds(pl.multiple_of((2 * index + core) * width, 128), width)


def part_of(where, owner, part):
    return pl.ds(pl.multiple_of(owner * part, 128), part)


def cut_shares(where, both, features, messages):
    for k, message in enumerate(messages, 1):
        part = message.shape[1] - features
        owner = lax.rem(where[1] + k, len(messages) + 1)
        message[:, :part] = both[:, part_of(where, owner, part)]
        message[:, part:] = both[:, features : 2 * features]


def fetch(where, rel, sources, targets, semaphores):
    from_in, from_out = sources
    weight_in, weight_out = targets
    copies = []
    for index in range(weight_in.shape[0]):
        cut = block_of(where, rel, index, weight_in.shape[2])
        for source, target in (
            (from_in.at[:, cut], weight_in.at[index]),
            (from_out.at[cut, :], weight_out.at[index]),
        ):
            copies.append(pltpu.make_async_copy(source, target, semaphores.at[len(copies)]))
            copies[-1].start()
    return copies


def fetch_kernel(where, ins, outs, scratch):
    for copy in fetch(where, 1, ins, outs, scratch[0]):
        copy.wait()


def other_kernel(where, ins, outs, scratch):
    *chunk, weight_in, weight_out = ins
    hidden, grad, both, *messages = outs
    features = weight_in.shape[1]
    both[:, :features] = chunk[0][...]
    both[:, features:] = chunk[1][...]
    cut_shares(where, both, features, messages)
    for index in range(weight_in.shape[0]):
        hidden[index] = dot(chunk[0][...], weight_in[index], 1, 0).astype(BF16)
        grad[index] = dot(chunk[1][...], weight_out[index], 1, 1).astype(BF16)


def own_kernel(where, ins, outs, scratch):
    both, *sources = ins
    copies = fetch(where, 0, sources, outs[:2], scratch[0])
    features = outs[0].shape[1]
    for index in range(outs[0].shape[0]):
        for which in range(2):
            copies[2 * index + which].wait()
            left = both[:, which * features : (which + 1) * features]
            outs[2 + which][index] = dot(left, outs[which][index], 1, which).astype(BF16)


def join_kernel(where, ins, outs, scratch):
    for which in range(2):
        total = ins[which][...].astype(F32) + ins[2 + which][...].astype(F32)
        outs[0][which] = total.astype(BF16)


def arrive_kernel(where, ins, outs, scratch):
    outs[0][...] = ins[0][...]
    for number, value in enumerate(ins[1:]):
        rows = value.shape[0]
        outs[1][number * rows : (number + 1) * rows, :] = value[...]


def lay(targets, which, index, value):
    rows = targets[0].shape[2]
    for number, target in enumerate(targets):
        target[which, index] = value[number * rows : (number + 1) * rows]


def hidden_kernel(keep, pieces, where, ins, outs, scratch):
    own, other, own_in, own_out, other_in, other_out = ins
    if keep:
        outs[-2][...] = other_in[...]
        outs[-1][...] = other_out[...]
    cut_shares(where, own, own_in.shape[1], outs[pieces : len(outs) - 2 * keep])
    features = own_in.shape[1]
    tokens, cotangents = slice(0, features), slice(features, 2 * features)
    for index in range(own_in.shape[0]):
        hidden = dot(own[:, tokens], own_in[index], 1, 0)
        hidden += dot(other[:, tokens], other_in[index], 1, 0)
        lay(outs[:pieces], 0, index, hidden.astype(BF16))
        grad = dot(own[:, cotangents], own_out[index], 1, 1)
        grad += dot(other[:, cotangents], other_out[index], 1, 1)
        lay(outs[:pieces], 1, index, grad.astype(BF16))


def gelu_kernel(n_depth, where, ins, outs, scratch):
    blocks = ins[0].shape[1]
    depth = where[1]
    for index in range(blocks):
        hidden, grad = ins[0][0, index].astype(F32), ins[0][1, index].astype(F32)
        for other in ins[1:]:
            hidden += other[0, index].astype(F32)
            grad += other[1, index].astype(F32)
        value, slope = gelu_parts(hidden)
        act, pre = value.astype(BF16), (grad * slope).astype(BF16)
        outs[0][0, index] = act
        outs[0][1, index] = pre
        for message in outs[1:]:
            message[index] = pre
    for k in range(1, len(outs)):
        owner = lax.rem(depth + k, n_depth) if k < n_depth else depth
        outs[k][blocks] = outs[0][0, owner]


def copy_kernel(where, ins, outs, scratch):
    outs[0][...] = ins[0][...]


def model_kernel(pieces, where, ins, outs, scratch):
    pairs, weights = ins[:pieces], ins[pieces:]
    pair = pairs[0]
    if pieces > 1:
        (pair,) = scratch
        rows = pairs[0].shape[2]
        for number, value in enumerate(pairs):
            pair[:, :, number * rows : (number + 1) * rows, :] = value[...]
    for rel, target in enumerate(outs):
        weight_in, weight_out = weights[2 * rel : 2 * rel + 2]
        out = grad = 0.0
        for index in range(pair.shape[1]):
            out += dot(pair[0, index], weight_out[index], 1, 0)
            grad += dot(pair[1, index], weight_in[index], 1, 1)
        target[0] = out.astype(BF16)
        target[1] = grad.astype(BF16)


def sum_kernel(where, ins, outs, scratch):
    for index in range(2):
        total = sum(value[index].astype(F32) for value in ins)
        if len(outs) == 1:
            outs[0][index] = total.astype(BF16)
        else:
            outs[index][...] = total.astype(BF16)


def early_kernel(near, where, ins, outs, scratch):
    all_tokens, all_cotangents, all_values = scratch
    own_in, own_out, other_in, other_out = outs
    blocks, part, width = own_in.shape
    features = own_out.shape[1]
    pairs, shares, came = ins[2 * near : 3 * near], ins[3 * near : 3 * near + 2], ins[3 * near + 2 :]
    rows = ins[0].shape[0]
    for rel in range(2):
        here = slice(rel * part, (rel + 1) * part)
        there = slice(rel * features, (rel + 1) * features)
        for number in range(near):
            at, source = slice(number * rows, (number + 1) * rows), ins[rel * near + number]
            all_tokens[at, here] = source[:, part_of(where, where[1], part)]
            all_cotangents[at, there] = source[:, features : 2 * features]
        for number in range(len(came)):
            at, source = slice(number * rows, (number + 1) * rows), shares[rel]
            start = (near + number) * rows
            all_tokens[start : start + rows, here] = source[at, :part]
            all_cotangents[start : start + rows, there] = source[at, part:]
    acts = [pair.at[0].at[where[1]] for pair in pairs] + [value.at[blocks] for value in came]
    pres = [[pair.at[1].at[index] for index in range(blocks)] for pair in pairs]
    pres += [[value.at[index] for index in range(blocks)] for value in came]

    def fill(sources):
        for number, source in enumerate(sources):
            all_values[number * rows : (number + 1) * rows, :] = source[...]

    for index in range(blocks):
        fill([value[index] for value in pres])
        term = dot(all_tokens[...], all_values[...], 0, 0)
        own_in[index] = term[:part]
        other_in[index] = term[part:].astype(BF16)
    fill(acts)
    term = dot(all_values[...], all_cotangents[...], 0, 0)
    own_out[...] = term[:, :features]
    other_out[...] = term[:, features:].astype(BF16)


def last_kernel(rel, groups, where, ins, outs, scratch):
    all_tokens, all_cotangents, all_values, held_in, held_out, semaphores = scratch
    own, *ins = ins
    shares, values, early = ins[: 2 * groups], ins[2 * groups : -2], ins[-2:]
    if rel:
        values, early = ins[2 * groups : -4], ins[-4:-2]
    rows, part = own.shape[0], all_tokens.shape[1]
    features, width = all_cotangents.shape[1], all_values.shape[1]
    blocks = held_in.shape[0]
    all_tokens[:rows, :] = own[:, part_of(where, where[1], part)]
    all_cotangents[:rows, :] = own[:, features : 2 * features]
    for number, share in enumerate(shares, 1):
        at = slice(number * rows, (number + 1) * rows)
        all_tokens[at, :] = share[:, :part]
        all_cotangents[at, :] = share[:, part:]
    copies = []

    def fill(index):
        row = 0
        for source in values:
            if len(source.shape) == 3:
                value = source[index]
            elif index < blocks:
                value = source[1, index]
            else:
                value = source[0, where[1]]
            all_values[row : row + value.shape[0], :] = value
            row += value.shape[0]

    def put(held, target, term):
        held[...] = term
        copies.append(pltpu.make_async_copy(held, target, semaphores.at[len(copies)]))
        copies[-1].start()

    core = where[0] if rel == 0 else 1 - where[0]
    fill(blocks)
    term = dot(all_values[...], all_cotangents[...], 0, 0) + early[1][...].astype(F32)
    at = pl.ds(pl.multiple_of(core * width, 128), width)
    put(held_out, outs[1].at[at, :], term)
    for index in range(blocks):
        fill(index)
        before = early[0][index].astype(F32)
        term = dot(all_tokens[...], all_values[...], 0, 0) + before
        put(held_in.at[index], outs[0].at[:, block_of(where, rel, index, width)], term)
    for copy in copies:
        copy.wait()


def shards(n_row, n_col, n_depth, tokens, weight_in, weight_out, output_grad):
    rows, features = tokens.shape
    part = features // n_depth
    blocks, width = n_depth, weight_in.shape[1] // (2 * n_depth)
    core = lax.axis_index("row") % 2
    depth = lax.axis_index("depth")
    chain = Chain(jnp.stack([core, depth]).astype(jnp.int32))

    def swap_cores(value):
        return lax.ppermute(value, "row", [(r, r ^ 1) for r in range(n_row)])

    def to_chip(value, k):
        return lax.ppermute(value, "row", [(r, (r + 2 * k) % n_row) for r in range(n_row)])

    def to_depth(value, k):
        return lax.ppermute(value, "depth", [(d, (d + k) % n_depth) for d in range(n_depth)])

    def to_col(value, k):
        return lax.ppermute(value, "col", [(c, (c + k) % n_col) for c in range(n_col)])

    single, pair_shape = shape(blocks, rows, width), shape(2, blocks, rows, width)
    model_shape = shape(2, rows, features)
    message_shape = shape(blocks + 1, rows, width)
    weight_shapes = [shape(blocks, features, width), shape(blocks, width, features)]
    groups = n_depth - 1
    last = n_col - 1
    own, other, shares = {}, {}, {}
    chip, crossed, pairs, came, model = {}, {}, {}, {}, {}

    def cross(stage):
        crossed[stage] = [
            [to_chip(value, k) for k in range(1, n_row // 2)] for value in chip[stage]
        ]

    ready = {}
    share_shapes = [shape(rows, part + features)] * groups
    semaphores = [pltpu.SemaphoreType.DMA((2 * blocks,))]

    def send_shares(stage, values):
        shares[stage] = [to_depth(value, k) for k, value in enumerate(values, 1)]
        ready["T", stage] = shares[stage]

    kept_weights = chain(
        fetch_kernel,
        [weight_in, weight_out],
        weight_shapes,
        scratch=semaphores,
        specs=[IN_HBM] * 2,
        limit=49,
    )
    other_weights = [swap_cores(value) for value in kept_weights]
    hidden, grad, own[0], *results = chain(
        other_kernel,
        [tokens, output_grad] + kept_weights,
        [single, single, shape(rows, 2 * features)] + share_shapes,
    )
    send_shares(0, results)
    swapped = [swap_cores(value) for value in (hidden, grad)]
    *own_weights, hidden, grad = chain(
        own_kernel,
        [own[0], weight_in, weight_out],
        weight_shapes + [single, single],
        scratch=semaphores,
        specs=[IN_VMEM] + [IN_HBM] * 2,
        limit=46,
    )
    chip[0] = chain(join_kernel, [hidden, grad] + swapped, [pair_shape])
    cross(0)
    other[0] = swap_cores(own[0])
    ready["O", 0] = [other[0]]
    own[1] = to_col(own[0], 1)
    raw, early_shares = {1: own[1]}, []

    def arrive_step(stage, after):
        raw[stage] = to_col(raw[stage - 1], 1)
        near, stacked = [raw[stage]], []
        if stage == last - 1:
            near += [value for earlier in range(stage) for value in shares[earlier]]
            stacked = [shape(stage * groups * rows, part + features)]
        own[stage], *results = chain(
            arrive_kernel, near, [shape(rows, 2 * features)] + stacked, after=after
        )
        if results:
            early_shares.extend(results + [swap_cores(results[0])])

    def hidden_step(stage, after):
        other[stage] = swap_cores(own[stage])
        sends = stage <= last - HOPS
        pieces = HALVES if stage == last else 1
        results = chain(
            functools.partial(hidden_kernel, stage == 1, pieces),
            [own[stage], other[stage]] + own_weights + other_weights,
            [shape(2, blocks, rows // pieces, width)] * pieces
            + (share_shapes if sends else [])
            + (weight_shapes if stage == 1 else []),
            after=after,
        )
        chip[stage], results = results[:pieces], results[pieces:]
        if sends:
            send_shares(stage, results[:groups])
        else:
            shares[stage] = [to_col(value, 1) for value in shares[stage - 1]]
            ready["T", stage] = shares[stage]
        if stage == 1:
            other_weights[:] = results[groups * sends :]
        cross(stage)

    def gelu_step(step, after):
        stage = min(step, last)
        piece = step - stage
        size = chip[stage][piece].shape[2]
        inputs = [chip[stage][piece]] + crossed[stage][piece]
        outputs = [shape(2, blocks, size, width)] + [shape(blocks + 1, size, width)] * groups
        if stage == last:
            outputs += [shape(blocks + 1, size, width)]
        pair, *messages = chain(
            functools.partial(gelu_kernel, n_depth), inputs, outputs, after=after
        )
        pairs.setdefault(stage, []).append(pair)
        arrived = [to_depth(value, k) for k, value in enumerate(messages[:groups], 1)]
        came.setdefault(stage, []).append(arrived)
        ready["Y", step] = arrived
        if stage == last:
            late.append(swap_cores(messages[groups]))

    def pass_step(stage, after):
        for value in came[last - 1][0]:
            (copied,) = chain(copy_kernel, [value], [message_shape], after=after)
            late_far.append(swap_cores(copied))
        ready["C", 0] = late_far[:]

    def model_step(stage, after):
        pieces = len(pairs[stage])
        mine, theirs = chain(
            functools.partial(model_kernel, pieces),
            pairs[stage] + own_weights + other_weights,
            [model_shape] * 2,
            after=after,
            scratch=[pltpu.VMEM(pair_shape.shape, BF16)] if pieces > 1 else [],
        )
        model[stage] = [mine, swap_cores(theirs)]
        ready["M", stage] = model[stage][1:]

    def sum_step(stage, after):
        brought = ring.get(stage - 1, []) if RING else []
        (total,) = chain(sum_kernel, model[stage] + brought, [model_shape], after=after)
        if RING:
            ring[stage] = [to_col(total, 1)]
        else:
            ring[stage] = [to_col(total, n_col - stage)]
        ready["S", stage] = ring[stage]

    def early_step(stage, after):
        count = rows * (last + (last - 1) * groups)
        term_sizes = [(blocks, part, width), (width, features)]
        near = list(range(last))
        values = [source[number] for source in (own, other) for number in near]
        values += [pairs[number][0] for number in near] + early_shares
        values += [value for number in range(last - 1) for value in came[number][0]]
        first_in, first_out, sent_in, sent_out = chain(
            functools.partial(early_kernel, last),
            values,
            [shape(*size, kind=kind) for kind in (F32, BF16) for size in term_sizes],
            after=after,
            scratch=[
                pltpu.VMEM((count, 2 * part), BF16),
                pltpu.VMEM((count, 2 * features), BF16),
                pltpu.VMEM((count, width), BF16),
            ],
            limit=24,
        )
        early.extend([first_in, first_out, swap_cores(sent_in), swap_cores(sent_out)])
        ready["E", 0] = early[2:]

    def last_step(rel, after):
        chunk = [own[last]] + shares[last - 1] + shares[last]
        arrived = [half[k] for k in range(groups) for half in came[last]]
        if rel == 0:
            values = pairs[last] + came[last - 1][0] + arrived
            swapped.extend(swap_cores(value) for value in arrived)
        else:
            values = late + late_far + swapped
        inputs = chunk + values + early[2 * rel : 2 * rel + 2] + results[2:]
        count = rows * (1 + 2 * groups)
        grads = [shape(part, 2 * blocks * width, kind=F32), shape(2 * width, features, kind=F32)]
        results[2:] = chain(
            functools.partial(last_kernel, rel, groups),
            inputs,
            grads,
            after=after,
            scratch=[
                pltpu.VMEM((count, part), BF16),
                pltpu.VMEM((count, features), BF16),
                pltpu.VMEM((count, width), BF16),
                pltpu.VMEM((blocks, part, width), F32),
                pltpu.VMEM((width, features), F32),
                pltpu.SemaphoreType.DMA((blocks + 1,)),
            ],
            specs=[IN_VMEM] * (len(inputs) - 2 * rel) + [IN_HBM] * (2 * rel),
            limit=20,
            to=IN_HBM,
            filled=2 * rel,
        )

    def final_step(stage, after):
        values = model[0] + (ring[last] if RING else [v for s in range(1, n_col) for v in ring[s]])
        results[:2] = chain(sum_kernel, values, [shape(rows, features)] * 2, after=after)

    ring, early, results = {}, [], [None, None]
    late, late_far, swapped = [], [], []
    steps = {
        "U": arrive_step,
        "H": hidden_step,
        "G": gelu_step,
        "C": pass_step,
        "M": model_step,
        "S": sum_step,
        "E": early_step,
        "L": last_step,
        "F": final_step,
    }
    order, waits = PLANS.get(last) or default_plan(last)
    for name, stage in order:
        chain.flops = COSTS.get((name, stage), 1000)
        steps[name](stage, [v for key in waits.get((name, stage), ()) for v in ready[key]])
    return tuple(results)


def plain_shards(tokens, weight_in, weight_out, output_grad):
    x_panel = lax.all_gather(tokens, "col", axis=0, tiled=True)
    dy_panel = lax.all_gather(output_grad, "col", axis=0, tiled=True)

    def hidden_total(term):
        return lax.psum(term.astype(BF16), "row").astype(F32)

    def scattered(term, axis):
        return lax.psum_scatter(term.astype(BF16), axis, scatter_dimension=0, tiled=True)

    value, slope = gelu_parts(hidden_total(dot(x_panel, weight_in, 1, 0)))
    act = value.astype(BF16)
    pre = (hidden_total(dot(dy_panel, weight_out, 1, 1)) * slope).astype(BF16)
    return (
        scattered(dot(act, weight_out, 1, 0), "col"),
        scattered(dot(pre, weight_in, 1, 1), "col"),
        scattered(dot(x_panel, pre, 0, 0), "depth").astype(F32),
        scattered(dot(act, dy_panel, 0, 0), "depth").astype(F32),
    )


def solution(mesh):
    placed = (
        P(("col", "depth"), "row"),
        P("row", "col"),
        P("col", "row"),
        P(("col", "depth"), "row"),
    )
    sizes = (mesh.shape["row"], mesh.shape["col"], mesh.shape["depth"])

    def local(tokens, weight_in, weight_out, output_grad):
        arrays = (tokens, weight_in, weight_out, output_grad)
        n_row, n_col, n_depth = sizes
        width, part = weight_in.shape[1] // (2 * n_depth), tokens.shape[1] // n_depth
        fits = width % 128 == 0 and part % 128 == 0 and tokens.shape[0] % (16 * HALVES) == 0
        if fits and n_row % 2 == 0 and n_col > 2 and n_depth > 1:
            return shards(*sizes, *arrays)
        return plain_shards(*arrays)

    return jax.shard_map(
        local,
        mesh=mesh,
        in_specs=placed,
        out_specs=(
            P(("col", "depth"), "row"),
            P(("col", "depth"), "row"),
            P(("row", "depth"), "col"),
            P(("col", "depth"), "row"),
        ),
        check_vma=False,
    )
```
